128 devices in a mesh: row: 16 (over y_hi, z, core), col: 8 (over y_lo, x).
Axes of the slice: x: 4, y: 4 (y_hi: 2, y_lo: 2; y = y_hi * 2 + y_lo), z: 4, core: 2. Of those that a mesh axis runs over, the one named last changes fastest.
Arguments:
- pair_rep: bfloat16 [1024, 1024, 128], P('row', 'col'), may hold values from -260 to 260
- labels: int32 [1024, 1024], P('row', 'col'), may hold values from 0 to 63
- residue_mask: int32 [1024], replicated, may hold values 0 or 1
- dist_weight: bfloat16 [128, 64], replicated, may hold values from -0.5 to 0.5
- dist_bias: float32 [64], replicated, may hold values from -4 to 4
- bias_weight: bfloat16 [128, 12], replicated, may hold values from -0.5 to 0.5
- query_scalar: bfloat16 [1024, 192], P('row'), may hold values from -6 to 6
- query_points: bfloat16 [1024, 144], P('row'), may hold values from -6 to 6
- key_scalar: bfloat16 [1024, 192], P('row'), may hold values from -6 to 6
- key_points: bfloat16 [1024, 144], P('row'), may hold values from -6 to 6
- value_scalar: bfloat16 [1024, 192], P('row'), may hold values from -6 to 6
- value_points: bfloat16 [1024, 288], P('row'), may hold values from -6 to 6
- point_weight: float32 [12], replicated, may hold values from -1 to 2
- cot_scalar: bfloat16 [1024, 192], P('row'), may hold values from -768 to 768
- cot_points: bfloat16 [1024, 288], P('row'), may hold values from -768 to 768
- cot_pair: bfloat16 [1024, 1536], P('row'), may hold values from -768 to 768
Outputs:
- pair_grad: bfloat16 [1024, 1024, 128], P('row', 'col')
- weight_grad: float32 [128, 64], replicated
The draws below stay inside these ranges and needn't reach their ends.
All inputs are finite; a program needn't handle non-finite values.
Results may differ from the reference program's by a relative error of at most 0.0052.
Values may be sent and summed in bfloat16 or wider, within the bound.
No kernel may reach another device: no remote copies, remote signals or barrier semaphores. Data moves between devices by JAX's collectives and lax.ppermute only.
A program may use at most 64 MiB of HBM per device.

```python
import math
import jax
import jax.numpy as jnp
from jax import lax

C = 128
BINS = 64
H = 12
DH = 16
QP = 4
VP = 8
L = 1024


def draw_pair_rep(key, part):
    key = jax.random.fold_in(key, 11)
    first = jax.random.fold_in(key, 0)
    return jnp.clip(jax.random.normal(first, (L, L, C), jnp.float32), -6.0, 6.0).astype(jnp.bfloat16)


def set_ends(drawn, key, low, top_value):
    shape = drawn.shape
    index_at = [jax.random.randint(jax.random.fold_in(key, axis), (), 0, shape[axis]) for axis in range(len(shape))]
    drawn = drawn.at[tuple(index_at)].set(low)
    longest = shape.index(max(shape))
    index_at[longest] = (index_at[longest] + 1) % shape[longest]
    return drawn.at[tuple(index_at)].set(top_value)


def level_of(own_key, extent, shards, smallest, high):
    level, own = 1.0, jax.random.fold_in(own_key, 6)
    for position, parts in shards:
        heights = jnp.exp(jax.random.uniform(jax.random.fold_in(own, position), (parts,), jnp.float32, smallest / len(shards), high / len(shards)))
        level = level * jnp.repeat(heights, extent[position] // parts).reshape([-1 if axis == position else 1 for axis in range(len(extent))])
    return level


def centred(key, shape, scale, bound, cuts=(), held_as=jnp.bfloat16):
    gain = level_of(key, shape, cuts, -0.22, 0.18) if cuts else 1.0
    entries = jax.random.normal(key, shape, jnp.float32) * scale * gain
    return jnp.minimum(jnp.maximum(entries, -bound), bound).astype(held_as)


def setup_inputs(seed: int = 0) -> dict:
    splits = jax.random.split(jax.random.key(seed), 17)
    pair_rep = draw_pair_rep(jax.random.fold_in(splits[16], 71), 0)
    labels = set_ends(jax.random.randint(splits[1], (L, L), 0, BINS), jax.random.fold_in(splits[1], 1), 0, BINS - 1).astype(jnp.int32)
    residue_mask = set_ends((jax.random.randint(splits[2], (L,), 0, 8) < 7).astype(jnp.int32), jax.random.fold_in(splits[2], 1), 0, 1)
    dist_weight = centred(splits[3], (C, BINS), C ** -0.5, 0.5)
    dist_bias = centred(splits[4], (BINS,), 1.0, 4.0, (), jnp.float32)
    bias_weight = centred(splits[5], (C, H), C ** -0.5, 0.5)
    query_scalar = centred(splits[6], (L, H * DH), 1.0, 6.0, ((0, 16),))
    query_points = centred(splits[7], (L, H * QP * 3), 1.0, 6.0, ((0, 16),))
    key_scalar = centred(splits[8], (L, H * DH), 1.0, 6.0, ((0, 16),))
    key_points = centred(splits[9], (L, H * QP * 3), 1.0, 6.0, ((0, 16),))
    value_scalar = centred(splits[10], (L, H * DH), 1.0, 6.0, ((0, 16),))
    value_points = centred(splits[11], (L, H * VP * 3), 1.0, 6.0, ((0, 16),))
    point_weight = jnp.clip(jax.random.uniform(splits[12], (H,), jnp.float32, -1.0, 2.0), -1.0, 2.0)
    cot_scalar = centred(splits[13], (L, H * DH), (L / 8), 768.0, ((0, 16),))
    cot_points = centred(splits[14], (L, H * VP * 3), (L / 8), 768.0, ((0, 16),))
    cot_pair = centred(splits[15], (L, H * C), (L / 8), 768.0, ((0, 16),))
    return dict(pair_rep=pair_rep, labels=labels, residue_mask=residue_mask, dist_weight=dist_weight, dist_bias=dist_bias, bias_weight=bias_weight, query_scalar=query_scalar, query_points=query_points, key_scalar=key_scalar, key_points=key_points, value_scalar=value_scalar, value_points=value_points, point_weight=point_weight, cot_scalar=cot_scalar, cot_points=cot_points, cot_pair=cot_pair)


logit_weight = math.sqrt(1.0 / 3.0)

def reference(pair_rep, labels, residue_mask, dist_weight, dist_bias, bias_weight, query_scalar, query_points, key_scalar, key_points, value_scalar, value_points, point_weight, cot_scalar, cot_points, cot_pair):
    block_rows = min(L, 128)
    block_count = L // block_rows
    mask_float = residue_mask.astype(jnp.float32)
    bin_iota = jnp.arange(BINS, dtype=jnp.int32)
    weight_flip = jnp.transpose(dist_weight)
    keys_all = key_scalar.reshape(L, H, DH).astype(jnp.float32)
    key_pts = key_points.reshape(L, H, QP * 3).astype(jnp.float32)
    value_rows = jnp.concatenate([value_scalar.reshape(L, H, DH), value_points.reshape(L, H, VP * 3)], axis=2).astype(jnp.float32)
    key_sq = jnp.transpose(lax.optimization_barrier(jnp.sum(jnp.square(key_pts), axis=2)))
    point_scale = jax.nn.softplus(point_weight) * (math.sqrt(2.0 / (9.0 * QP)) / 2.0)
    key_bias = jnp.where(mask_float > 0, 0.0, -1000000000.0)
    bias_float = bias_weight.astype(jnp.float32)

    def one_block(weight_acc, block_index):
        offset = (block_index * block_rows).astype(jnp.int32)
        own_rows = lax.dynamic_slice_in_dim(pair_rep, offset, block_rows, 0)
        mirror_rows = jnp.transpose(lax.dynamic_slice_in_dim(pair_rep, offset, block_rows, 1), (1, 0, 2))
        logits = jnp.dot(own_rows, dist_weight, preferred_element_type=jnp.float32) + jnp.dot(mirror_rows, dist_weight, preferred_element_type=jnp.float32) + dist_bias
        probabilities = jax.nn.softmax(logits, axis=-1)
        own_mask = lax.dynamic_slice_in_dim(mask_float, offset, block_rows, 0)
        valid_pairs = (own_mask[:, None] * mask_float[None, :])[:, :, None]
        own_labels = lax.dynamic_slice_in_dim(labels, offset, block_rows, 0)
        mirror_labels = jnp.transpose(lax.dynamic_slice_in_dim(labels, offset, block_rows, 1))
        grad_bins = (valid_pairs * (probabilities - (own_labels[:, :, None] == bin_iota).astype(jnp.float32))).astype(jnp.bfloat16)
        grad_mirror = (valid_pairs * (probabilities - (mirror_labels[:, :, None] == bin_iota).astype(jnp.float32))).astype(jnp.bfloat16)
        dist_grad = jnp.dot(grad_bins, weight_flip, preferred_element_type=jnp.float32) + jnp.dot(grad_mirror, weight_flip, preferred_element_type=jnp.float32)
        flat_bins = grad_bins.reshape(-1, BINS)
        weight_term = jnp.dot(jnp.transpose(own_rows.reshape(-1, C)), flat_bins, preferred_element_type=jnp.float32) + jnp.dot(jnp.transpose(mirror_rows.reshape(-1, C)), flat_bins, preferred_element_type=jnp.float32)
        queries = lax.dynamic_slice_in_dim(query_scalar, offset, block_rows, 0).reshape(block_rows, H, DH).astype(jnp.float32)
        query_pts = lax.dynamic_slice_in_dim(query_points, offset, block_rows, 0).reshape(block_rows, H, QP * 3).astype(jnp.float32)
        scalar_term = jnp.einsum('ihd,jhd->hij', queries, keys_all)
        cross_term = jnp.einsum('ihd,jhd->hij', query_pts, key_pts)
        query_sq = jnp.transpose(lax.optimization_barrier(jnp.sum(jnp.square(query_pts), axis=2)))[:, :, None]
        squared_gap = query_sq + key_sq[:, None, :] - 2.0 * cross_term
        rows_float = own_rows.astype(jnp.float32)
        pair_bias = jnp.einsum('ijc,ch->hij', rows_float, bias_float)
        attn_logits = logit_weight * (scalar_term * (1.0 / math.sqrt(DH)) + pair_bias - point_scale[:, None, None] * squared_gap) + key_bias[None, None, :]
        attention = jax.nn.softmax(attn_logits, axis=-1)
        attention_half = attention.astype(jnp.bfloat16)
        cot_values = jnp.concatenate([lax.dynamic_slice_in_dim(cot_scalar, offset, block_rows, 0).reshape(block_rows, H, DH), lax.dynamic_slice_in_dim(cot_points, offset, block_rows, 0).reshape(block_rows, H, VP * 3)], axis=2).astype(jnp.float32)
        pair_cot = lax.dynamic_slice_in_dim(cot_pair, offset, block_rows, 0).reshape(block_rows, H, C).astype(jnp.float32)
        value_grad = jnp.einsum('ihd,jhd->hij', cot_values, value_rows) + jnp.einsum('ihc,ijc->hij', pair_cot, rows_float)
        row_total = lax.optimization_barrier(jnp.sum(attention * value_grad, axis=-1, keepdims=True))
        logit_grad = (attention * (value_grad - row_total)).astype(jnp.bfloat16)
        ipa_grad = jnp.einsum('hij,ihc->ijc', attention_half.astype(jnp.float32), pair_cot) + logit_weight * jnp.einsum('hij,ch->ijc', logit_grad.astype(jnp.float32), bias_float)
        block_out = (dist_grad + ipa_grad).astype(jnp.bfloat16)
        return (weight_acc + weight_term, block_out)
    weight_grad, blocks_out = lax.scan(one_block, jnp.zeros((C, BINS), jnp.float32), jnp.arange(block_count, dtype=jnp.int32))
    return (blocks_out.reshape(L, L, C), weight_grad)
```

```python
import functools
import math

import jax
import jax.numpy as jnp
import numpy as np
from jax import lax
from jax.experimental import pallas as pl
from jax.experimental.pallas import tpu as pltpu
from jax.sharding import PartitionSpec as P

AXES = ("row", "col")
LOGIT_WEIGHT = math.sqrt(1.0 / 3.0)
HEADS = 12
PAD_HEADS = 16
CHUNK = 8
QUANT = 32760.0

WIDTHS = (192, 144, 192, 288)
PER_HEAD = (16, 12, 16, 24)
CAT = 896
WINDOWS = ((0, 256), (128, 384), (256, 896))

NT = (((1,), (1,)), ((), ()))
TN = (((0,), (0,)), ((), ()))

CHIPS = [(x, y, z) for x in range(4) for y in range(4) for z in range(4)]
Y_SWAP = (0, 2, 1, 3)


def device_index(chip, core):
    x, y, z = chip
    return ((y // 2) * 8 + z * 2 + core) * 8 + (y % 2) * 4 + x


def mirror_chip(chip):
    x, y, z = chip
    return (z, Y_SWAP[y], x)


def halfway_chip(chip, core):
    x, y, z = chip
    if core == 0:
        return (x, y, (3 * x + 3 * z + 2) % 4)
    return (x, Y_SWAP[y], (3 * x + 3 * z) % 4)


FIRST_HOP = [(device_index(n, h), device_index(halfway_chip(n, h), h)) for n in CHIPS for h in (0, 1)]
SECOND_HOP = [
    [
        (device_index(halfway_chip(n, h), h), device_index(mirror_chip(n), (h + s) % 2))
        for n in CHIPS
        for h in (0, 1)
    ]
    for s in (0, 1)
]
MIRROR = [(device_index(n, h), device_index(mirror_chip(n), h)) for n in CHIPS for h in (0, 1)]
CORE_SWAP = [(device_index(n, h), device_index(n, 1 - h)) for n in CHIPS for h in (0, 1)]


def shift_map(axis, distance):
    pairs = []
    for n in CHIPS:
        m = list(n)
        m[axis] = (m[axis] + distance) % 4
        pairs += [(device_index(n, h), device_index(tuple(m), h)) for h in (0, 1)]
    return pairs


def head_masks():
    masks = np.zeros((3, PAD_HEADS, CAT), np.float32)
    start = 0
    for part, (width, size) in enumerate(zip(WIDTHS, PER_HEAD)):
        for column in range(width):
            masks[min(part, 2), column // size, start + column] = 1.0
        start += width
    return [masks[k][:, lo:hi] for k, (lo, hi) in enumerate(WINDOWS)]


def dot(a, b, dims=(((1,), (0,)), ((), ()))):
    return lax.dot_general(a, b, dims, preferred_element_type=jnp.float32)


def eye(n, dtype):
    return (
        lax.broadcasted_iota(jnp.int32, (n, n), 0) == lax.broadcasted_iota(jnp.int32, (n, n), 1)
    ).astype(dtype)


def flipped(weight, rows):
    k = weight.shape[1]
    pick = (
        lax.broadcasted_iota(jnp.int32, (rows, k), 0) == lax.broadcasted_iota(jnp.int32, (rows, k), 1)
    ).astype(jnp.bfloat16)
    return dot(pick, weight, NT).astype(jnp.bfloat16)


def own_core():
    return lax.rem(lax.axis_index("row"), 2)


def logits_kernel(pair_ref, weight_ref, labels_ref, own_ref, same_ref, other_ref, slabs, top):
    step = pl.program_id(0)
    weight_t = flipped(weight_ref[...], 64)
    flat = pair_ref[...].reshape(CHUNK * 128, 128)
    terms = dot(weight_t, flat, NT)
    for t in range(CHUNK):
        term = terms[:, t * 128 : (t + 1) * 128]
        row = step * CHUNK + t
        own_ref[t] = term
        slabs[pl.ds(row, 64, stride=64), :] = term
        top[pl.ds(row, 1), :] = jnp.max(jnp.abs(term), axis=0, keepdims=True)

    @pl.when(step == pl.num_programs(0) - 1)
    def _():
        core = own_core()
        level = jnp.ceil(16.0 * jnp.log2(jnp.maximum(top[...], 1e-30)))
        scale = jnp.exp2(level * (-1.0 / 16.0)) * QUANT

        def put(slab, upper, lower):
            turned = jnp.transpose(jnp.concatenate([upper, lower], axis=0))
            first, second = turned[:64], turned[64:]
            same_ref[slab] = narrow(jnp.where(core == 0, first, second))
            other_ref[slab] = narrow(jnp.where(core == 0, second, first))

        def narrow(values):
            return jnp.clip(jnp.round(values), -32767.0, 32767.0).astype(jnp.int32).astype(jnp.int16)

        def pair_of_bins(b, carry):
            upper = slabs[pl.ds(pl.multiple_of(b * 64, 64), 64), :] * scale
            lower = slabs[pl.ds(pl.multiple_of((b + 32) * 64, 64), 64), :] * scale
            put(b, upper, lower)
            return carry

        lax.fori_loop(0, 32, pair_of_bins, 0)
        put(32, level, labels_ref[...].astype(jnp.float32))


def own_logits(pair_tile, dist_weight, labels):
    rows = pair_tile.shape[0]
    block = jax.ShapeDtypeStruct((33, 64, 128), jnp.int16)
    whole = lambda *shape: pl.BlockSpec(shape, lambda i: (0,) * len(shape))
    return pl.pallas_call(
        logits_kernel,
        grid=(rows // CHUNK,),
        in_specs=[
            pl.BlockSpec((CHUNK, 128, 128), lambda i: (i, 0, 0)),
            whole(128, 64),
            whole(64, 128),
        ],
        out_specs=[
            pl.BlockSpec((CHUNK, 64, 128), lambda i: (i, 0, 0)),
            whole(33, 64, 128),
            whole(33, 64, 128),
        ],
        out_shape=[jax.ShapeDtypeStruct((rows, 64, 128), jnp.float32), block, block],
        scratch_shapes=[pltpu.VMEM((64 * 64, 128), jnp.float32), pltpu.VMEM((64, 128), jnp.float32)],
        compiler_params=pltpu.CompilerParams(vmem_limit_bytes=32 * 1024 * 1024),
        cost_estimate=pl.CostEstimate(flops=200_000_000, bytes_accessed=6_000_000, transcendentals=8192),
        name="own_logits",
    )(pair_tile, dist_weight, labels)


def attention_kernel(
    pair_ref, cat_ref, near_ref, far_ref, cot_ref, bias_ref, point_ref, mask_ref, scalar_mask_ref, point_mask_ref,
    value_mask_ref, exp_ref, grad_ref, cot_out_ref, stats_ref, keys, cot_rows,
):
    step = pl.program_id(0)
    length = CHUNK * PAD_HEADS

    @pl.when(step == 0)
    def _():
        core = own_core()
        near, far = near_ref[...].astype(jnp.float32), far_ref[...].astype(jnp.float32)
        keys[:64] = jnp.where(core == 0, near, far).astype(jnp.bfloat16)
        keys[64:] = jnp.where(core == 0, far, near).astype(jnp.bfloat16)
        for h in range(HEADS):
            cot_rows[h * 64 : (h + 1) * 64] = cot_ref[:, h * 128 : (h + 1) * 128]

    def iota(shape, dim):
        return lax.broadcasted_iota(jnp.int32, shape, dim)

    residue = step * CHUNK + iota((length, 64), 0) // PAD_HEADS
    pick = (residue == iota((length, 64), 1)).astype(jnp.bfloat16)
    spread = dot(pick, cat_ref[...])
    left = []
    for (lo, hi), mask in zip(WINDOWS, (scalar_mask_ref, point_mask_ref, value_mask_ref)):
        head_columns = jnp.concatenate([mask[...]] * CHUNK, axis=0)
        left.append(spread[:, lo:hi] * head_columns)
    right = [keys[:, lo:hi] for lo, hi in WINDOWS]
    scalar_term, cross_term, value_term = [dot(a.astype(jnp.bfloat16), b, NT) for a, b in zip(left, right)]
    query_sq = jnp.sum(left[1] * left[1], axis=1, keepdims=True)
    key_points = right[1].astype(jnp.float32)
    key_sq = lax.dot_general(
        point_mask_ref[...],
        key_points * key_points,
        NT,
        precision=lax.Precision.HIGHEST,
        preferred_element_type=jnp.float32,
    )
    key_sq = jnp.concatenate([key_sq] * CHUNK, axis=0)

    row_of = iota((length, 768), 0)
    column_of = iota((length, 768), 1)
    cot_pick = (step * CHUNK + row_of // PAD_HEADS == column_of % 64) & (row_of % PAD_HEADS == column_of // 64)
    cot = dot(cot_pick.astype(jnp.bfloat16), cot_rows[...]).astype(jnp.bfloat16)
    cot_out_ref[...] = cot.reshape(CHUNK, PAD_HEADS, 128)

    bias_t = flipped(bias_ref[...], PAD_HEADS)
    pair_bias, pair_value = [], []
    for t in range(CHUNK):
        both = jnp.concatenate([bias_t, cot[t * PAD_HEADS : (t + 1) * PAD_HEADS]], axis=0)
        result = dot(both, pair_ref[t], NT)
        pair_bias.append(result[:PAD_HEADS])
        pair_value.append(result[PAD_HEADS:])
    pair_bias = jnp.concatenate(pair_bias, axis=0)
    value_grad = value_term + jnp.concatenate(pair_value, axis=0)

    head_of = iota((length, 128), 0) % PAD_HEADS
    raw = jnp.sum(jnp.where(head_of == iota((length, 128), 1), point_ref[...], 0.0), axis=1, keepdims=True)
    softplus = jnp.maximum(raw, 0.0) + jnp.log1p(jnp.exp(-jnp.abs(raw)))
    point_scale = softplus * (math.sqrt(2.0 / 36.0) / 2.0)

    column_mask = mask_ref[pl.ds(lax.axis_index("col"), 1), :]
    key_bias = jnp.where(column_mask > 0, 0.0, -1000000000.0)
    logits = (
        LOGIT_WEIGHT
        * (scalar_term * 0.25 + pair_bias - point_scale * (query_sq + key_sq - 2.0 * cross_term))
        + key_bias
    )
    top = jnp.max(logits, axis=1, keepdims=True)
    weights = jnp.exp(logits - top)
    total = jnp.sum(weights, axis=1, keepdims=True)
    weighted = jnp.sum(weights * value_grad, axis=1, keepdims=True)
    exp_ref[...] = weights.reshape(CHUNK, PAD_HEADS, 128)
    grad_ref[...] = value_grad.reshape(CHUNK, PAD_HEADS, 128)
    lane = iota((length, 128), 1)
    packed = jnp.where(lane == 0, top, jnp.where(lane == 1, total, jnp.where(lane == 2, weighted, 0.0)))
    packed = jnp.transpose(packed)
    for q in range(3):
        stats_ref[pl.ds(q * 8 + step, 1), :] = packed[q : q + 1]


def attention_parts(pair_tile, cat, near, far, cot_pair, bias_weight, point_row, mask_rows):
    rows = pair_tile.shape[0]
    whole = lambda *shape: pl.BlockSpec(shape, lambda i: (0,) * len(shape))
    part = pl.BlockSpec((CHUNK, PAD_HEADS, 128), lambda i: (i, 0, 0))
    masks = [jnp.asarray(m) for m in head_masks()]
    return pl.pallas_call(
        attention_kernel,
        grid=(rows // CHUNK,),
        in_specs=[
            pl.BlockSpec((CHUNK, 128, 128), lambda i: (i, 0, 0)),
            whole(64, CAT),
            whole(64, CAT),
            whole(64, CAT),
            whole(64, 1536),
            whole(128, HEADS),
            whole(1, 128),
            whole(8, 128),
        ]
        + [whole(*m.shape) for m in masks],
        out_specs=[part, part, part, whole(24, 128)],
        out_shape=[
            jax.ShapeDtypeStruct((rows, PAD_HEADS, 128), jnp.float32),
            jax.ShapeDtypeStruct((rows, PAD_HEADS, 128), jnp.float32),
            jax.ShapeDtypeStruct((rows, PAD_HEADS, 128), jnp.bfloat16),
            jax.ShapeDtypeStruct((24, 128), jnp.float32),
        ],
        scratch_shapes=[pltpu.VMEM((128, CAT), jnp.bfloat16), pltpu.VMEM((768, 128), jnp.bfloat16)],
        compiler_params=pltpu.CompilerParams(vmem_limit_bytes=32 * 1024 * 1024),
        cost_estimate=pl.CostEstimate(flops=1_000_000_000, bytes_accessed=4_000_000, transcendentals=200_000),
        name="attention_parts",
    )(pair_tile, cat, near, far, cot_pair, bias_weight, point_row, mask_rows, *masks)


def bins_kernel(
    mask_smem, pair_ref, own_ref, near_ref, far_ref, labels_ref, bias_ref, mask_ref, bins_ref, weight_ref, mirror,
    mirror_labels,
):
    step = pl.program_id(0)

    @pl.when(step == 0)
    def _():
        core = own_core()
        low_lanes = lax.broadcasted_iota(jnp.int32, (64, 128), 1) < 64

        def halves(slab):
            near = near_ref[slab].astype(jnp.int32).astype(jnp.float32)
            far = far_ref[slab].astype(jnp.int32).astype(jnp.float32)
            first = jnp.where(core == 0, near, far)
            second = jnp.where(core == 0, far, near)
            upper = jnp.where(low_lanes, first, pltpu.roll(second, 64, 1))
            lower = jnp.where(low_lanes, pltpu.roll(first, 64, 1), second)
            return upper, lower

        level, other_labels = halves(32)
        mirror_labels[...] = other_labels
        scale = jnp.exp2(level * (1.0 / 16.0)) * (1.0 / QUANT)

        def pair_of_bins(b, carry):
            upper, lower = halves(b)
            mirror[pl.ds(pl.multiple_of(b * 64, 64), 64), :] = upper * scale
            mirror[pl.ds(pl.multiple_of((b + 32) * 64, 64), 64), :] = lower * scale
            return carry

        lax.fori_loop(0, 32, pair_of_bins, 0)
        weight_ref[...] = jnp.zeros_like(weight_ref)

    bias = jnp.sum(eye(64, jnp.float32) * bias_ref[...], axis=1, keepdims=True)
    column_mask = mask_ref[pl.ds(lax.axis_index("col"), 1), :].astype(jnp.float32)
    bin_of = lax.broadcasted_iota(jnp.int32, (64, 128), 0)
    first_row = lax.axis_index("row") * 64
    grads = []
    for t in range(CHUNK):
        row = step * CHUNK + t
        logits = own_ref[t] + mirror[pl.ds(row, 64, stride=64), :] + bias
        weights = jnp.exp(logits - jnp.max(logits, axis=0, keepdims=True))
        valid = column_mask * mask_smem[first_row + row].astype(jnp.float32)
        share = 2.0 * valid / jnp.sum(weights, axis=0, keepdims=True)
        own_label = labels_ref[pl.ds(row, 1), :]
        other_label = mirror_labels[pl.ds(row, 1), :].astype(jnp.int32)
        hits = jnp.where(bin_of == own_label, valid, 0.0) + jnp.where(bin_of == other_label, valid, 0.0)
        grad = (weights * share - hits).astype(jnp.bfloat16)
        bins_ref[t] = grad
        grads.append(grad)
    flat = pair_ref[...].reshape(CHUNK * 128, 128)
    weight_ref[...] += dot(jnp.concatenate(grads, axis=1), flat)


def bin_gradient(pair_tile, own, near, far, labels, dist_bias, mask_rows, residue_mask):
    rows = pair_tile.shape[0]
    whole = lambda *shape: pl.BlockSpec(shape, lambda i: (0,) * len(shape))
    return pl.pallas_call(
        bins_kernel,
        grid=(rows // CHUNK,),
        in_specs=[
            pl.BlockSpec(memory_space=pltpu.SMEM),
            pl.BlockSpec((CHUNK, 128, 128), lambda i: (i, 0, 0)),
            pl.BlockSpec((CHUNK, 64, 128), lambda i: (i, 0, 0)),
            whole(33, 64, 128),
            whole(33, 64, 128),
            whole(64, 128),
            whole(1, 64),
            whole(8, 128),
        ],
        out_specs=[pl.BlockSpec((CHUNK, 64, 128), lambda i: (i, 0, 0)), whole(64, 128)],
        out_shape=[
            jax.ShapeDtypeStruct((rows, 64, 128), jnp.bfloat16),
            jax.ShapeDtypeStruct((64, 128), jnp.float32),
        ],
        scratch_shapes=[pltpu.VMEM((64 * 64, 128), jnp.float32), pltpu.VMEM((64, 128), jnp.float32)],
        compiler_params=pltpu.CompilerParams(vmem_limit_bytes=32 * 1024 * 1024),
        cost_estimate=pl.CostEstimate(flops=200_000_000, bytes_accessed=6_000_000, transcendentals=600_000),
        name="bin_gradient",
    )(residue_mask, pair_tile, own, near, far, labels, dist_bias, mask_rows)


def output_kernel(exp_ref, grad_ref, stats_ref, bins_ref, cot_ref, weight_ref, bias_ref, out_ref):
    step = pl.program_id(0)
    length = CHUNK * PAD_HEADS
    tops = [stats_ref[c, pl.ds(step, 1), :] for c in range(8)]
    totals = [stats_ref[c, pl.ds(8 + step, 1), :] for c in range(8)]
    weighted = [stats_ref[c, pl.ds(16 + step, 1), :] for c in range(8)]
    top = functools.reduce(jnp.maximum, tops)
    factors = [jnp.exp(m - top) for m in tops]
    total = sum(f * s for f, s in zip(factors, totals))
    mean = sum(f * s for f, s in zip(factors, weighted)) / total
    own_top = stats_ref[lax.axis_index("col"), pl.ds(step, 1), :]
    share = jnp.exp(own_top - top) / total
    share = jnp.transpose(jnp.broadcast_to(share, (length, 128)))
    mean = jnp.transpose(jnp.broadcast_to(mean, (length, 128)))
    attention = exp_ref[...].reshape(length, 128) * share
    logit_grad = attention * (grad_ref[...].reshape(length, 128) - mean)
    attention = attention.astype(jnp.bfloat16)
    logit_grad = (logit_grad * LOGIT_WEIGHT).astype(jnp.bfloat16)
    weight_t = flipped(weight_ref[...], 64)
    bias_t = flipped(bias_ref[...], PAD_HEADS)
    for t in range(CHUNK):
        rows = slice(t * PAD_HEADS, (t + 1) * PAD_HEADS)
        left = jnp.concatenate([bins_ref[t], attention[rows], logit_grad[rows]], axis=0)
        right = jnp.concatenate([weight_t, cot_ref[t], bias_t], axis=0)
        out_ref[t] = dot(left, right, TN).astype(jnp.bfloat16)


def pair_gradient(weights, value_grad, stats, bins, cot, dist_weight, bias_weight):
    rows = bins.shape[0]
    whole = lambda *shape: pl.BlockSpec(shape, lambda i: (0,) * len(shape))
    part = pl.BlockSpec((CHUNK, PAD_HEADS, 128), lambda i: (i, 0, 0))
    return pl.pallas_call(
        output_kernel,
        grid=(rows // CHUNK,),
        in_specs=[
            part,
            part,
            whole(8, 24, 128),
            pl.BlockSpec((CHUNK, 64, 128), lambda i: (i, 0, 0)),
            part,
            whole(128, 64),
            whole(128, HEADS),
        ],
        out_specs=pl.BlockSpec((CHUNK, 128, 128), lambda i: (i, 0, 0)),
        out_shape=jax.ShapeDtypeStruct((rows, 128, 128), jnp.bfloat16),
        compiler_params=pltpu.CompilerParams(vmem_limit_bytes=32 * 1024 * 1024),
        cost_estimate=pl.CostEstimate(flops=300_000_000, bytes_accessed=5_000_000, transcendentals=10_000),
        name="pair_gradient",
    )(weights, value_grad, stats, bins, cot, dist_weight, bias_weight)


def sum_over_devices(term):
    term = term + lax.ppermute(term, AXES, CORE_SWAP)
    for axis in range(3):
        one, two, three = [lax.ppermute(term, AXES, shift_map(axis, d)) for d in (1, 2, 3)]
        term = (term + two) + (one + three)
    return term


def body(
    pair_rep,
    labels,
    residue_mask,
    dist_weight,
    dist_bias,
    bias_weight,
    query_scalar,
    query_points,
    key_scalar,
    key_points,
    value_scalar,
    value_points,
    point_weight,
    cot_scalar,
    cot_points,
    cot_pair,
):
    pad = jnp.zeros((query_scalar.shape[0], CAT - sum(WIDTHS)), jnp.bfloat16)
    own_keys = jnp.concatenate([key_scalar, key_points, value_scalar, value_points, pad], axis=1)
    near_keys = lax.ppermute(own_keys, AXES, MIRROR)
    far_keys = lax.ppermute(near_keys, AXES, CORE_SWAP)
    cat = jnp.concatenate([query_scalar, query_points, cot_scalar, cot_points, pad], axis=1)
    mask_rows = residue_mask.reshape(8, 128)
    point_row = jnp.concatenate([point_weight, jnp.zeros((128 - HEADS,), jnp.float32)]).reshape(1, 128)

    own, same, other = own_logits(pair_rep, dist_weight, labels)
    same = lax.ppermute(same, AXES, FIRST_HOP)
    other = lax.ppermute(other, AXES, FIRST_HOP)
    same = lax.ppermute(same, AXES, SECOND_HOP[0])
    other = lax.ppermute(other, AXES, SECOND_HOP[1])

    weights, value_grad, cot, stats = attention_parts(
        pair_rep, cat, near_keys, far_keys, cot_pair, bias_weight, point_row, mask_rows
    )
    stats = lax.all_to_all(
        jnp.broadcast_to(stats[None], (8,) + stats.shape), "col", split_axis=0, concat_axis=0, tiled=True
    )
    bins, weight_term = bin_gradient(
        pair_rep, own, same, other, labels, dist_bias.reshape(1, 64), mask_rows, residue_mask
    )
    weight_grad = jnp.transpose(sum_over_devices(weight_term))
    pair_grad = pair_gradient(weights, value_grad, stats, bins, cot, dist_weight, bias_weight)
    return (pair_grad, weight_grad)


def solution(mesh):
    placed = (
        P("row", "col", None),
        P("row", "col"),
        P(),
        P(),
        P(),
        P(),
        P("row", None),
        P("row", None),
        P("row", None),
        P("row", None),
        P("row", None),
        P("row", None),
        P(),
        P("row", None),
        P("row", None),
        P("row", None),
    )
    return jax.shard_map(
        body, mesh=mesh, in_specs=placed, out_specs=(P("row", "col", None), P()), check_vma=False
    )
```

```python
import functools
import math

import jax
import jax.numpy as jnp
import numpy as np
from jax import lax
from jax.experimental import pallas as pl
from jax.experimental.pallas import tpu as pltpu
from jax.sharding import PartitionSpec as P

AXES = ("row", "col")
LOGIT_WEIGHT = math.sqrt(1.0 / 3.0)
HEADS = 12
PAD_HEADS = 16
CHUNK = 8
QUANT = 32760.0

WIDTHS = (192, 144, 192, 288)
PER_HEAD = (16, 12, 16, 24)
CAT = 896
WINDOWS = ((0, 256), (128, 384), (256, 896))

NT = (((1,), (1,)), ((), ()))
TN = (((0,), (0,)), ((), ()))

CHIPS = [(x, y, z) for x in range(4) for y in range(4) for z in range(4)]
Y_SWAP = (0, 2, 1, 3)


def device_index(chip, core):
    x, y, z = chip
    return ((y // 2) * 8 + z * 2 + core) * 8 + (y % 2) * 4 + x


def mirror_chip(chip):
    x, y, z = chip
    return (z, Y_SWAP[y], x)


def halfway_chip(chip, core):
    x, y, z = chip
    if core == 0:
        return (x, y, (x + z) % 4)
    return ((x + 3 * z + 2) % 4, Y_SWAP[y], x)


FIRST_HOP = [(device_index(n, h), device_index(halfway_chip(n, h), h)) for n in CHIPS for h in (0, 1)]
SECOND_HOP = [
    [
        (device_index(halfway_chip(n, h), h), device_index(mirror_chip(n), (h + s) % 2))
        for n in CHIPS
        for h in (0, 1)
    ]
    for s in (0, 1)
]
MIRROR = [(device_index(n, h), device_index(mirror_chip(n), h)) for n in CHIPS for h in (0, 1)]
CORE_SWAP = [(device_index(n, h), device_index(n, 1 - h)) for n in CHIPS for h in (0, 1)]


Y_PAIR = [(device_index((x, y, z), h), device_index((x, y ^ 1, z), h)) for x, y, z in CHIPS for h in (0, 1)]


def shift_map(axis, distance):
    pairs = []
    for n in CHIPS:
        m = list(n)
        m[axis] = (m[axis] + distance) % 4
        pairs += [(device_index(n, h), device_index(tuple(m), h)) for h in (0, 1)]
    return pairs


def head_masks():
    masks = np.zeros((3, PAD_HEADS, CAT), np.float32)
    start = 0
    for part, (width, size) in enumerate(zip(WIDTHS, PER_HEAD)):
        for column in range(width):
            masks[min(part, 2), column // size, start + column] = 1.0
        start += width
    return [masks[k][:, lo:hi] for k, (lo, hi) in enumerate(WINDOWS)]


def dot(a, b, dims=(((1,), (0,)), ((), ()))):
    return lax.dot_general(a, b, dims, preferred_element_type=jnp.float32)


def eye(n, dtype):
    return (
        lax.broadcasted_iota(jnp.int32, (n, n), 0) == lax.broadcasted_iota(jnp.int32, (n, n), 1)
    ).astype(dtype)


def padded_heads(bias_ref):
    heads = bias_ref.shape[0]
    pick = (
        lax.broadcasted_iota(jnp.int32, (PAD_HEADS, heads), 0)
        == lax.broadcasted_iota(jnp.int32, (PAD_HEADS, heads), 1)
    ).astype(jnp.bfloat16)
    return dot(pick, bias_ref[...]).astype(jnp.bfloat16)


def own_core():
    return lax.rem(lax.axis_index("row"), 2)


def lay_out(cat_ref, parts):
    start = 0
    for part in parts:
        width = part.shape[1]
        cat_ref[:, start : start + width] = part[...]
        start += width
    cat_ref[:, start:] = jnp.zeros((cat_ref.shape[0], cat_ref.shape[1] - start), cat_ref.dtype)


def chunk_copies(source, target, arrived):
    count = arrived.shape[0]
    size = source.shape[0] // count
    return [
        pltpu.make_async_copy(
            source.at[pl.ds(k * size, size)], target.at[pl.ds(k * size, size)], arrived.at[k]
        )
        for k in range(count)
    ]


HBM = pl.BlockSpec(memory_space=pltpu.HBM)
VMEM = pl.BlockSpec(memory_space=pltpu.VMEM)
SMEM = pl.BlockSpec(memory_space=pltpu.SMEM)
PARAMS = pltpu.CompilerParams(vmem_limit_bytes=16 * 1024 * 1024)


def logits_kernel(
    pair_hbm, weight_hbm, labels_hbm, own_hbm, same_ref, other_ref, pair_ref, weight_ref, labels_ref, own_ref, slabs,
    top, pair_sem, own_sem, small_sem,
):
    small = [
        pltpu.make_async_copy(weight_hbm, weight_ref, small_sem.at[0]),
        pltpu.make_async_copy(labels_hbm, labels_ref, small_sem.at[1]),
    ]
    coming = chunk_copies(pair_hbm, pair_ref, pair_sem)
    going = chunk_copies(own_ref, own_hbm, own_sem)
    small[0].start()
    coming[0].start()
    for copy in coming[1:] + small[1:]:
        copy.start()
    small[0].wait()
    weight_t = weight_ref[...]
    size = pair_ref.shape[0] // len(coming)
    for k in range(len(coming)):
        coming[k].wait()
        for first in range(k * size, (k + 1) * size, 4):
            flat = pair_ref[first : first + 4].reshape(4 * 128, 128)
            terms = dot(weight_t, flat, NT)
            for t in range(4):
                term = terms[:, t * 128 : (t + 1) * 128]
                row = first + t
                own_ref[row] = term
                slabs[pl.ds(row, 64, stride=64), :] = term
                top[pl.ds(row, 1), :] = jnp.max(jnp.abs(term), axis=0, keepdims=True)
        going[k].start()
    small[1].wait()

    core = own_core()
    level = jnp.ceil(16.0 * jnp.log2(jnp.maximum(top[...], 1e-30)))
    scale = jnp.exp2(level * (-1.0 / 16.0)) * QUANT

    def narrow(values):
        return jnp.clip(jnp.round(values), -32767.0, 32767.0).astype(jnp.int32).astype(jnp.int16)

    def put(slab, upper, lower):
        turned = jnp.transpose(jnp.concatenate([upper, lower], axis=0))
        first, second = turned[:64], turned[64:]
        same_ref[slab] = narrow(jnp.where(core == 0, first, second))
        other_ref[slab] = narrow(jnp.where(core == 0, second, first))

    def pair_of_bins(b, carry):
        upper = slabs[pl.ds(pl.multiple_of(b * 64, 64), 64), :] * scale
        lower = slabs[pl.ds(pl.multiple_of((b + 32) * 64, 64), 64), :] * scale
        put(b, upper, lower)
        return carry

    lax.fori_loop(0, 32, pair_of_bins, 0, unroll=8)
    put(32, level, labels_ref[...].astype(jnp.float32))
    for copy in going:
        copy.wait()


def own_logits(pair_tile, weight_rows, labels):
    rows = pair_tile.shape[0]
    block = jax.ShapeDtypeStruct((33, 64, 128), jnp.int16)
    return pl.pallas_call(
        logits_kernel,
        in_specs=[HBM] * 3,
        out_specs=[HBM, VMEM, VMEM],
        out_shape=[
            jax.ShapeDtypeStruct((rows, 64, 128), jnp.float32),
            block,
            block,
        ],
        scratch_shapes=[
            pltpu.VMEM(pair_tile.shape, jnp.bfloat16),
            pltpu.VMEM(weight_rows.shape, jnp.bfloat16),
            pltpu.VMEM(labels.shape, jnp.int32),
            pltpu.VMEM((rows, 64, 128), jnp.float32),
            pltpu.VMEM((64 * 64, 128), jnp.float32),
            pltpu.VMEM((64, 128), jnp.float32),
            pltpu.SemaphoreType.DMA((8,)),
            pltpu.SemaphoreType.DMA((8,)),
            pltpu.SemaphoreType.DMA((2,)),
        ],
        compiler_params=pltpu.CompilerParams(vmem_limit_bytes=60 * 1024 * 1024),
        cost_estimate=pl.CostEstimate(flops=200_000_000, bytes_accessed=6_000_000, transcendentals=8192),
        name="own_logits",
    )(pair_tile, weight_rows, labels)


def attention_kernel(point_smem, pair_ref, near_ref, far_ref, cot_ref, bias_ref, mask_ref, *refs):
    scalar_mask_ref, point_mask_ref, value_mask_ref = refs[:3]
    query_refs = refs[3:7]
    exp_ref, grad_ref, cot_out_ref, stats_ref, keys, cot_rows, cat_ref = refs[7:]
    length = CHUNK * PAD_HEADS

    def iota(shape, dim):
        return lax.broadcasted_iota(jnp.int32, shape, dim)

    core = own_core()
    near, far = near_ref[...].astype(jnp.float32), far_ref[...].astype(jnp.float32)
    keys[:64] = jnp.where(core == 0, near, far).astype(jnp.bfloat16)
    keys[64:] = jnp.where(core == 0, far, near).astype(jnp.bfloat16)
    lay_out(cat_ref, query_refs)
    for h in range(HEADS):
        cot_rows[h * 64 : (h + 1) * 64] = cot_ref[:, h * 128 : (h + 1) * 128]
    bias_t = padded_heads(bias_ref)

    right = [keys[:, lo:hi] for lo, hi in WINDOWS]
    key_points = right[1].astype(jnp.float32)
    key_sq = lax.dot_general(
        point_mask_ref[...],
        key_points * key_points,
        NT,
        precision=lax.Precision.HIGHEST,
        preferred_element_type=jnp.float32,
    )
    key_sq = jnp.concatenate([key_sq] * CHUNK, axis=0)
    head_masks = [
        jnp.concatenate([mask[...]] * CHUNK, axis=0) for mask in (scalar_mask_ref, point_mask_ref, value_mask_ref)
    ]

    head_of = iota((length, 128), 0) % PAD_HEADS
    raw = jnp.zeros((length, 128), jnp.float32)
    for h in range(HEADS):
        raw = jnp.where(head_of == h, point_smem[h], raw)
    softplus = jnp.maximum(raw, 0.0) + jnp.log1p(jnp.exp(-jnp.abs(raw)))
    point_scale = softplus * (math.sqrt(2.0 / 36.0) / 2.0)
    column_mask = mask_ref[pl.ds(lax.axis_index("col"), 1), :]
    key_bias = jnp.where(column_mask > 0, 0.0, -1000000000.0)
    lane = iota((length, 128), 1)

    for step in range(pair_ref.shape[0] // CHUNK):
        residue = step * CHUNK + iota((length, 64), 0) // PAD_HEADS
        pick = (residue == iota((length, 64), 1)).astype(jnp.bfloat16)
        spread = dot(pick, cat_ref[...])
        left = [spread[:, lo:hi] * mask for (lo, hi), mask in zip(WINDOWS, head_masks)]
        scalar_term, cross_term, value_term = [dot(a.astype(jnp.bfloat16), b, NT) for a, b in zip(left, right)]
        query_sq = jnp.sum(left[1] * left[1], axis=1, keepdims=True)

        row_of = iota((length, 768), 0)
        column_of = iota((length, 768), 1)
        cot_pick = (step * CHUNK + row_of // PAD_HEADS == column_of % 64) & (row_of % PAD_HEADS == column_of // 64)
        cot = dot(cot_pick.astype(jnp.bfloat16), cot_rows[...]).astype(jnp.bfloat16)
        rows = slice(step * CHUNK, (step + 1) * CHUNK)
        cot_out_ref[rows] = cot.reshape(CHUNK, PAD_HEADS, 128)

        pair_bias, pair_value = [], []
        for t in range(CHUNK):
            both = jnp.concatenate([bias_t, cot[t * PAD_HEADS : (t + 1) * PAD_HEADS]], axis=0)
            result = dot(both, pair_ref[step * CHUNK + t], NT)
            pair_bias.append(result[:PAD_HEADS])
            pair_value.append(result[PAD_HEADS:])
        pair_bias = jnp.concatenate(pair_bias, axis=0)
        value_grad = value_term + jnp.concatenate(pair_value, axis=0)

        logits = (
            LOGIT_WEIGHT
            * (scalar_term * 0.25 + pair_bias - point_scale * (query_sq + key_sq - 2.0 * cross_term))
            + key_bias
        )
        top = jnp.max(logits, axis=1, keepdims=True)
        weights = jnp.exp(logits - top)
        total = jnp.sum(weights, axis=1, keepdims=True)
        weighted = jnp.sum(weights * value_grad, axis=1, keepdims=True)
        exp_ref[rows] = weights.reshape(CHUNK, PAD_HEADS, 128)
        grad_ref[rows] = value_grad.reshape(CHUNK, PAD_HEADS, 128)
        packed = jnp.where(lane == 0, top, jnp.where(lane == 1, total, jnp.where(lane == 2, weighted, 0.0)))
        packed = jnp.transpose(packed)
        for q in range(3):
            stats_ref[q * 8 + step : q * 8 + step + 1, :] = packed[q : q + 1]


def attention_parts(pair_tile, queries, near, far, cot_pair, bias_rows, point_weight, mask_rows):
    rows = pair_tile.shape[0]
    masks = [jnp.asarray(m) for m in head_masks()]
    return pl.pallas_call(
        attention_kernel,
        in_specs=[SMEM] + [VMEM] * (6 + len(masks) + len(queries)),
        out_specs=[VMEM] * 4,
        out_shape=[
            jax.ShapeDtypeStruct((rows, PAD_HEADS, 128), jnp.float32),
            jax.ShapeDtypeStruct((rows, PAD_HEADS, 128), jnp.float32),
            jax.ShapeDtypeStruct((rows, PAD_HEADS, 128), jnp.bfloat16),
            jax.ShapeDtypeStruct((24, 128), jnp.float32),
        ],
        scratch_shapes=[
            pltpu.VMEM((128, CAT), jnp.bfloat16),
            pltpu.VMEM((768, 128), jnp.bfloat16),
            pltpu.VMEM((64, CAT), jnp.bfloat16),
        ],
        compiler_params=PARAMS,
        cost_estimate=pl.CostEstimate(flops=1_000_000_000, bytes_accessed=4_000_000, transcendentals=200_000),
        name="attention_parts",
    )(point_weight, pair_tile, near, far, cot_pair, bias_rows, mask_rows, *masks, *queries)


def bins_kernel(
    mask_smem, pair_ref, own_ref, labels_ref, near_ref, far_ref, bias_ref, mask_ref, bins_ref, weight_ref, mirror,
    mirror_labels,
):
    core = own_core()
    low_lanes = lax.broadcasted_iota(jnp.int32, (64, 128), 1) < 64

    def halves(slab):
        near = near_ref[slab].astype(jnp.int32).astype(jnp.float32)
        far = far_ref[slab].astype(jnp.int32).astype(jnp.float32)
        first = jnp.where(core == 0, near, far)
        second = jnp.where(core == 0, far, near)
        upper = jnp.where(low_lanes, first, pltpu.roll(second, 64, 1))
        lower = jnp.where(low_lanes, pltpu.roll(first, 64, 1), second)
        return upper, lower

    level, other_labels = halves(32)
    mirror_labels[...] = other_labels
    scale = jnp.exp2(level * (1.0 / 16.0)) * (1.0 / QUANT)

    def pair_of_bins(b, carry):
        upper, lower = halves(b)
        mirror[pl.ds(pl.multiple_of(b * 64, 64), 64), :] = upper * scale
        mirror[pl.ds(pl.multiple_of((b + 32) * 64, 64), 64), :] = lower * scale
        return carry

    lax.fori_loop(0, 32, pair_of_bins, 0, unroll=8)
    bias = jnp.sum(eye(64, jnp.float32) * bias_ref[...], axis=1, keepdims=True)
    bias = jnp.broadcast_to(bias, (64, 128))
    column_mask = mask_ref[pl.ds(lax.axis_index("col"), 1), :].astype(jnp.float32)
    bin_of = lax.broadcasted_iota(jnp.int32, (64, 128), 0)
    first_row = lax.axis_index("row") * 64

    total = jnp.zeros((64, 128), jnp.float32)
    for step in range(pair_ref.shape[0] // CHUNK):
        grads = []
        for t in range(CHUNK):
            row = step * CHUNK + t
            logits = own_ref[row] + mirror[pl.ds(row, 64, stride=64), :] + bias
            weights = jnp.exp(logits - jnp.max(logits, axis=0, keepdims=True))
            valid = column_mask * mask_smem[first_row + row].astype(jnp.float32)
            share = 2.0 * valid / jnp.sum(weights, axis=0, keepdims=True)
            own_label = labels_ref[pl.ds(row, 1), :]
            other_label = mirror_labels[pl.ds(row, 1), :].astype(jnp.int32)
            hits = jnp.where(bin_of == own_label, valid, 0.0) + jnp.where(bin_of == other_label, valid, 0.0)
            grad = (weights * share - hits).astype(jnp.bfloat16)
            bins_ref[row] = grad
            grads.append(grad)
        flat = pair_ref[step * CHUNK : (step + 1) * CHUNK].reshape(CHUNK * 128, 128)
        total += dot(jnp.concatenate(grads, axis=1), flat)
    weight_ref[...] = total


def bin_gradient(pair_tile, own, near, far, labels, dist_bias, mask_rows, residue_mask):
    rows = pair_tile.shape[0]
    return pl.pallas_call(
        bins_kernel,
        in_specs=[SMEM] + [VMEM] * 7,
        out_specs=[VMEM, VMEM],
        out_shape=[
            jax.ShapeDtypeStruct((rows, 64, 128), jnp.bfloat16),
            jax.ShapeDtypeStruct((64, 128), jnp.float32),
        ],
        scratch_shapes=[
            pltpu.VMEM((64 * 64, 128), jnp.float32),
            pltpu.VMEM((64, 128), jnp.float32),
        ],
        compiler_params=PARAMS,
        cost_estimate=pl.CostEstimate(flops=200_000_000, bytes_accessed=6_000_000, transcendentals=600_000),
        name="bin_gradient",
    )(residue_mask, pair_tile, own, labels, near, far, dist_bias, mask_rows)


def output_kernel(exp_ref, grad_ref, *refs):
    stats_refs, (bins_ref, cot_ref, weight_ref, bias_ref, out_hbm, out_ref, sent) = refs[:4], refs[4:]
    length = CHUNK * PAD_HEADS
    weight_t = weight_ref[...]
    bias_t = padded_heads(bias_ref)
    places = [(ref, y) for ref in stats_refs for y in (0, 1)]
    tops = [ref[y, 0:8, :] for ref, y in places]
    totals = [ref[y, 8:16, :] for ref, y in places]
    weighted = [ref[y, 16:24, :] for ref, y in places]
    top = functools.reduce(jnp.maximum, tops)
    factors = [jnp.exp(m - top) for m in tops]
    total = sum(f * s for f, s in zip(factors, totals))
    means = sum(f * s for f, s in zip(factors, weighted)) / total
    shares = factors[0] / total
    going = chunk_copies(out_ref, out_hbm, sent)
    for step in range(out_ref.shape[0] // CHUNK):
        share = jnp.transpose(jnp.broadcast_to(shares[step : step + 1], (length, 128)))
        mean = jnp.transpose(jnp.broadcast_to(means[step : step + 1], (length, 128)))
        rows = slice(step * CHUNK, (step + 1) * CHUNK)
        attention = exp_ref[rows].reshape(length, 128) * share
        logit_grad = attention * (grad_ref[rows].reshape(length, 128) - mean)
        attention = attention.astype(jnp.bfloat16)
        logit_grad = (logit_grad * LOGIT_WEIGHT).astype(jnp.bfloat16)
        for t in range(CHUNK):
            heads = slice(t * PAD_HEADS, (t + 1) * PAD_HEADS)
            row = step * CHUNK + t
            left = jnp.concatenate([bins_ref[row], attention[heads], logit_grad[heads]], axis=0)
            right = jnp.concatenate([weight_t, cot_ref[row], bias_t], axis=0)
            out_ref[row] = dot(left, right, TN).astype(jnp.bfloat16)
        going[step].start()
    for copy in going:
        copy.wait()


def pair_gradient(weights, value_grad, stats, bins, cot, weight_rows, bias_rows):
    rows = bins.shape[0]
    return pl.pallas_call(
        output_kernel,
        in_specs=[VMEM] * 10,
        out_specs=HBM,
        out_shape=jax.ShapeDtypeStruct((rows, 128, 128), jnp.bfloat16),
        scratch_shapes=[
            pltpu.VMEM((rows, 128, 128), jnp.bfloat16),
            pltpu.SemaphoreType.DMA((rows // CHUNK,)),
        ],
        compiler_params=PARAMS,
        cost_estimate=pl.CostEstimate(flops=300_000_000, bytes_accessed=5_000_000, transcendentals=10_000),
        name="pair_gradient",
    )(weights, value_grad, *stats, bins, cot, weight_rows, bias_rows)


def sum_over_devices(term):
    term = term + lax.ppermute(term, AXES, CORE_SWAP)
    for axis in range(3):
        one, two, three = [lax.ppermute(term, AXES, shift_map(axis, d)) for d in (1, 2, 3)]
        term = (term + two) + (one + three)
    return term


def body(
    pair_rep,
    labels,
    residue_mask,
    dist_weight,
    dist_bias,
    bias_weight,
    query_scalar,
    query_points,
    key_scalar,
    key_points,
    value_scalar,
    value_points,
    point_weight,
    cot_scalar,
    cot_points,
    cot_pair,
):
    mask_rows = residue_mask.reshape(8, 128)
    weight_rows = jnp.transpose(dist_weight)
    bias_rows = jnp.transpose(bias_weight)

    pad = jnp.zeros((query_scalar.shape[0], CAT - sum(WIDTHS)), jnp.bfloat16)
    own_keys = jnp.concatenate([key_scalar, key_points, value_scalar, value_points, pad], axis=1)
    near_keys = lax.ppermute(own_keys, AXES, MIRROR)
    own, same, other = own_logits(pair_rep, weight_rows, labels)
    same, other, near_keys = lax.optimization_barrier((same, other, near_keys))
    same = lax.ppermute(same, AXES, FIRST_HOP)
    other = lax.ppermute(other, AXES, FIRST_HOP)
    far_keys = lax.ppermute(near_keys, AXES, CORE_SWAP)
    weights, value_grad, cot, stats = attention_parts(
        pair_rep,
        (query_scalar, query_points, cot_scalar, cot_points),
        near_keys,
        far_keys,
        cot_pair,
        bias_rows,
        point_weight,
        mask_rows,
    )
    same, other, stats = lax.optimization_barrier((same, other, stats))
    same = lax.ppermute(same, AXES, SECOND_HOP[0])
    other = lax.ppermute(other, AXES, SECOND_HOP[1])
    two_stats = jnp.stack([stats, lax.ppermute(stats, AXES, Y_PAIR)])
    stats = [two_stats] + [lax.ppermute(two_stats, AXES, shift_map(0, d)) for d in (1, 2, 3)]
    same, other, stats = lax.optimization_barrier((same, other, stats))
    bins, weight_term = bin_gradient(
        pair_rep, own, same, other, labels, dist_bias.reshape(1, 64), mask_rows, residue_mask
    )
    weight_grad = jnp.transpose(sum_over_devices(weight_term))
    pair_grad = pair_gradient(weights, value_grad, stats, bins, cot, weight_rows, bias_rows)
    return (pair_grad, weight_grad)


def solution(mesh):
    placed = (
        P("row", "col", None),
        P("row", "col"),
        P(),
        P(),
        P(),
        P(),
        P("row", None),
        P("row", None),
        P("row", None),
        P("row", None),
        P("row", None),
        P("row", None),
        P(),
        P("row", None),
        P("row", None),
        P("row", None),
    )
    return jax.shard_map(
        body, mesh=mesh, in_specs=placed, out_specs=(P("row", "col", None), P()), check_vma=False
    )
```

```python
import functools
import math

import jax
import jax.numpy as jnp
import numpy as np
from jax import lax
from jax.experimental import pallas as pl
from jax.experimental.pallas import tpu as pltpu
from jax.sharding import PartitionSpec as P

AXES = ("row", "col")
LOGIT_WEIGHT = math.sqrt(1.0 / 3.0)
HEADS = 12
PAD_HEADS = 16
CHUNK = 8
QUANT = 32760.0
BINS = 64
STATS = 24

WIDTHS = (192, 144, 192, 288)
PER_HEAD = (16, 12, 16, 24)
CAT = 896
WINDOWS = ((0, 256), (128, 384), (256, 896))
WINDOW_PARTS = ((0,), (1,), (2, 3))

NT = (((1,), (1,)), ((), ()))
TN = (((0,), (0,)), ((), ()))

CHIPS = [(x, y, z) for x in range(4) for y in range(4) for z in range(4)]
Y_SWAP = (0, 2, 1, 3)


def device_index(chip, core):
    x, y, z = chip
    return ((y // 2) * 8 + z * 2 + core) * 8 + (y % 2) * 4 + x


def mirror_chip(chip):
    x, y, z = chip
    return (z, Y_SWAP[y], x)


def halfway_chip(chip, core):
    x, y, z = chip
    if core == 0:
        return (x, y, (x + z) % 4)
    return ((x + 3 * z + 2) % 4, Y_SWAP[y], x)


FIRST_HOP = [(device_index(n, h), device_index(halfway_chip(n, h), h)) for n in CHIPS for h in (0, 1)]
SECOND_HOP = [
    [
        (device_index(halfway_chip(n, h), h), device_index(mirror_chip(n), (h + s) % 2))
        for n in CHIPS
        for h in (0, 1)
    ]
    for s in (0, 1)
]
MIRROR = [(device_index(n, h), device_index(mirror_chip(n), h)) for n in CHIPS for h in (0, 1)]
CORE_SWAP = [(device_index(n, h), device_index(n, 1 - h)) for n in CHIPS for h in (0, 1)]


def trade_map(axis, bits):
    pairs = []
    for n in CHIPS:
        m = list(n)
        m[axis] ^= bits
        pairs += [(device_index(n, h), device_index(tuple(m), h)) for h in (0, 1)]
    return pairs


def head_columns(lo, hi, parts):
    head = lax.broadcasted_iota(jnp.int32, (PAD_HEADS, hi - lo), 0)
    column = lax.broadcasted_iota(jnp.int32, (PAD_HEADS, hi - lo), 1) + lo
    held = jnp.zeros((PAD_HEADS, hi - lo), jnp.float32)
    for part in parts:
        size = PER_HEAD[part]
        first = sum(WIDTHS[:part]) + head * size
        inside = (column >= first) & (column < first + size) & (head < HEADS)
        held = jnp.where(inside, 1.0, held)
    return held


def dot(a, b, dims=(((1,), (0,)), ((), ()))):
    return lax.dot_general(a, b, dims, preferred_element_type=jnp.float32)


def eye(n, dtype):
    return (
        lax.broadcasted_iota(jnp.int32, (n, n), 0) == lax.broadcasted_iota(jnp.int32, (n, n), 1)
    ).astype(dtype)


def padded_heads(bias_ref):
    heads = bias_ref.shape[0]
    pick = (
        lax.broadcasted_iota(jnp.int32, (PAD_HEADS, heads), 0)
        == lax.broadcasted_iota(jnp.int32, (PAD_HEADS, heads), 1)
    ).astype(jnp.bfloat16)
    return dot(pick, bias_ref[...]).astype(jnp.bfloat16)


def own_core():
    return lax.rem(lax.axis_index("row"), 2)


def lay_out(cat_ref, parts):
    start = 0
    for part in parts:
        width = part.shape[1]
        cat_ref[:, start : start + width] = part[...]
        start += width
    cat_ref[:, start:] = jnp.zeros((cat_ref.shape[0], cat_ref.shape[1] - start), cat_ref.dtype)


def chunk_copies(source, target, arrived):
    count = arrived.shape[0]
    size = source.shape[0] // count
    return [
        pltpu.make_async_copy(
            source.at[pl.ds(k * size, size)], target.at[pl.ds(k * size, size)], arrived.at[k]
        )
        for k in range(count)
    ]


HBM = pl.BlockSpec(memory_space=pltpu.HBM)
VMEM = pl.BlockSpec(memory_space=pltpu.VMEM)
SMEM = pl.BlockSpec(memory_space=pltpu.SMEM)
PARAMS = pltpu.CompilerParams(vmem_limit_bytes=16 * 1024 * 1024)


SLABS = 33
SLAB_PARTS = ((0, 8), (8, 16), (16, 24), (24, 33))


def logits_kernel(pair_hbm, weight_hbm, labels_hbm, *refs):
    keys_hbm, (own_hbm, same_hbm, other_hbm, cat_hbm) = refs[:4], refs[4:8]
    pair_ref, weight_ref, labels_ref, own_ref, same_ref, other_ref, cat_ref, slabs, top = refs[8:17]
    pair_sem, own_sem, slab_sem, small_sem = refs[17:21]
    keys_refs = refs[21:]
    copy = pltpu.make_async_copy
    weight_in = copy(weight_hbm, weight_ref, small_sem.at[0])
    small_in = [copy(labels_hbm, labels_ref, small_sem.at[1])]
    small_in += [copy(a, b, small_sem.at[3 + k]) for k, (a, b) in enumerate(zip(keys_hbm, keys_refs))]
    cat_out = copy(cat_ref, cat_hbm, small_sem.at[2])
    pair_in = chunk_copies(pair_hbm, pair_ref, pair_sem)
    own_out = chunk_copies(own_ref, own_hbm, own_sem)
    weight_in.start()
    for c in pair_in + small_in:
        c.start()
    weight_in.wait()
    weight_t = weight_ref[...]
    size = pair_ref.shape[0] // len(pair_in)
    for k in range(len(pair_in)):
        pair_in[k].wait()
        for first in range(k * size, (k + 1) * size, 4):
            flat = pair_ref[first : first + 4].reshape(4 * 128, 128)
            terms = dot(weight_t, flat, NT)
            for t in range(4):
                term = terms[:, t * 128 : (t + 1) * 128]
                row = first + t
                own_ref[row] = term
                slabs[pl.ds(row, 64, stride=64), :] = term
                top[pl.ds(row, 1), :] = jnp.max(jnp.abs(term), axis=0, keepdims=True)
        own_out[k].start()
    for c in small_in:
        c.wait()
    lay_out(cat_ref, keys_refs)
    cat_out.start()

    core = own_core()
    level = jnp.ceil(16.0 * jnp.log2(jnp.maximum(top[...], 1e-30)))
    scale = jnp.exp2(level * (-1.0 / 16.0)) * QUANT

    def narrow(values):
        return jnp.clip(jnp.round(values), -32767.0, 32767.0).astype(jnp.int32).astype(jnp.int16)

    def put(slab, upper, lower):
        turned = jnp.transpose(jnp.concatenate([upper, lower], axis=0))
        first, second = turned[:64], turned[64:]
        same_ref[slab] = narrow(jnp.where(core == 0, first, second))
        other_ref[slab] = narrow(jnp.where(core == 0, second, first))

    slab_out = []
    for part, (lo, hi) in enumerate(SLAB_PARTS):
        for b in range(lo, min(hi, 32)):
            put(b, slabs[b * 64 : (b + 1) * 64, :] * scale, slabs[(b + 32) * 64 : (b + 33) * 64, :] * scale)
        if hi == SLABS:
            put(32, level, labels_ref[...].astype(jnp.float32))
        for k, (ref, hbm) in enumerate(((same_ref, same_hbm), (other_ref, other_hbm))):
            slab_out.append(copy(ref.at[pl.ds(lo, hi - lo)], hbm.at[pl.ds(lo, hi - lo)], slab_sem.at[part, k]))
            slab_out[-1].start()
    for c in own_out + slab_out + [cat_out]:
        c.wait()


def own_logits(pair_tile, weight_rows, labels, keys):
    rows = pair_tile.shape[0]
    block = jax.ShapeDtypeStruct((SLABS, 64, 128), jnp.int16)
    cat = jax.ShapeDtypeStruct((rows, CAT), jnp.bfloat16)
    own = jax.ShapeDtypeStruct((rows, 64, 128), jnp.float32)
    arrays = [pair_tile, weight_rows, labels, own, block, block, cat]
    return pl.pallas_call(
        logits_kernel,
        in_specs=[HBM] * (3 + len(keys)),
        out_specs=[HBM] * 4,
        out_shape=[own, block, block, cat],
        scratch_shapes=[pltpu.VMEM(a.shape, a.dtype) for a in arrays]
        + [
            pltpu.VMEM((64 * 64, 128), jnp.float32),
            pltpu.VMEM((64, 128), jnp.float32),
            pltpu.SemaphoreType.DMA((8,)),
            pltpu.SemaphoreType.DMA((8,)),
            pltpu.SemaphoreType.DMA((len(SLAB_PARTS), 2)),
            pltpu.SemaphoreType.DMA((3 + len(keys),)),
        ]
        + [pltpu.VMEM(k.shape, k.dtype) for k in keys],
        compiler_params=pltpu.CompilerParams(vmem_limit_bytes=60 * 1024 * 1024),
        cost_estimate=pl.CostEstimate(flops=200_000_000, bytes_accessed=6_000_000, transcendentals=8192),
        name="own_logits",
    )(pair_tile, weight_rows, labels, *keys)


def pair_parts_kernel(pair_ref, cot_ref, bias_ref, bias_out_ref, value_out_ref, cot_out_ref, cot_rows):
    length = CHUNK * PAD_HEADS
    for h in range(HEADS):
        cot_rows[h * 64 : (h + 1) * 64] = cot_ref[:, h * 128 : (h + 1) * 128]
    bias_t = padded_heads(bias_ref)
    row_of = lax.broadcasted_iota(jnp.int32, (length, 768), 0)
    column_of = lax.broadcasted_iota(jnp.int32, (length, 768), 1)
    same_head = row_of % PAD_HEADS == column_of // 64
    place = column_of % 64 - row_of // PAD_HEADS
    for step in range(pair_ref.shape[0] // CHUNK):
        pick = (same_head & (place == step * CHUNK)).astype(jnp.bfloat16)
        cot = dot(pick, cot_rows[...]).astype(jnp.bfloat16)
        cot_out_ref[step * CHUNK : (step + 1) * CHUNK] = cot.reshape(CHUNK, PAD_HEADS, 128)
        for t in range(CHUNK):
            row = step * CHUNK + t
            both = jnp.concatenate([bias_t, cot[t * PAD_HEADS : (t + 1) * PAD_HEADS]], axis=0)
            result = dot(both, pair_ref[row], NT)
            bias_out_ref[row] = result[:PAD_HEADS]
            value_out_ref[row] = result[PAD_HEADS:]


def pair_parts(pair_tile, cot_pair, bias_rows):
    rows = pair_tile.shape[0]
    part = jax.ShapeDtypeStruct((rows, PAD_HEADS, 128), jnp.float32)
    return pl.pallas_call(
        pair_parts_kernel,
        in_specs=[VMEM] * 3,
        out_specs=[VMEM] * 3,
        out_shape=[part, part, jax.ShapeDtypeStruct((rows, PAD_HEADS, 128), jnp.bfloat16)],
        scratch_shapes=[pltpu.VMEM((768, 128), jnp.bfloat16)],
        compiler_params=PARAMS,
        cost_estimate=pl.CostEstimate(flops=1_000_000_000, bytes_accessed=4_000_000, transcendentals=0),
        name="pair_parts",
    )(pair_tile, cot_pair, bias_rows)


def attention_kernel(point_smem, near_ref, far_ref, pair_bias_ref, pair_value_ref, mask_ref, *refs):
    query_refs = refs[:4]
    exp_ref, grad_ref, stats_ref, keys, cat_ref = refs[4:]
    length = CHUNK * PAD_HEADS

    def iota(shape, dim):
        return lax.broadcasted_iota(jnp.int32, shape, dim)

    core = own_core()
    near, far = near_ref[...].astype(jnp.float32), far_ref[...].astype(jnp.float32)
    keys[:64] = jnp.where(core == 0, near, far).astype(jnp.bfloat16)
    keys[64:] = jnp.where(core == 0, far, near).astype(jnp.bfloat16)
    lay_out(cat_ref, query_refs)

    masks = [head_columns(lo, hi, parts) for (lo, hi), parts in zip(WINDOWS, WINDOW_PARTS)]
    right = [keys[:, lo:hi] for lo, hi in WINDOWS]
    key_points = right[1].astype(jnp.float32)
    key_sq = lax.dot_general(
        masks[1],
        key_points * key_points,
        NT,
        precision=lax.Precision.HIGHEST,
        preferred_element_type=jnp.float32,
    )
    key_sq = jnp.concatenate([key_sq] * CHUNK, axis=0)
    masks = [jnp.concatenate([mask] * CHUNK, axis=0) for mask in masks]

    head_of = iota((length, 128), 0) % PAD_HEADS
    raw = jnp.zeros((length, 128), jnp.float32)
    for h in range(HEADS):
        raw = jnp.where(head_of == h, point_smem[h], raw)
    softplus = jnp.maximum(raw, 0.0) + jnp.log1p(jnp.exp(-jnp.abs(raw)))
    point_scale = softplus * (math.sqrt(2.0 / 36.0) / 2.0)
    column_mask = mask_ref[pl.ds(lax.axis_index("col"), 1), :]
    key_bias = jnp.where(column_mask > 0, 0.0, -1000000000.0)
    lane = iota((length, 128), 1)
    place = iota((length, 64), 1) - iota((length, 64), 0) // PAD_HEADS

    for step in range(exp_ref.shape[0] // CHUNK):
        pick = (place == step * CHUNK).astype(jnp.bfloat16)
        spread = dot(pick, cat_ref[...])
        left = [spread[:, lo:hi] * mask for (lo, hi), mask in zip(WINDOWS, masks)]
        scalar_term, cross_term, value_term = [dot(a.astype(jnp.bfloat16), b, NT) for a, b in zip(left, right)]
        query_sq = jnp.sum(left[1] * left[1], axis=1, keepdims=True)
        rows = slice(step * CHUNK, (step + 1) * CHUNK)
        pair_bias = pair_bias_ref[rows].reshape(length, 128)
        value_grad = value_term + pair_value_ref[rows].reshape(length, 128)
        logits = (
            LOGIT_WEIGHT
            * (scalar_term * 0.25 + pair_bias - point_scale * (query_sq + key_sq - 2.0 * cross_term))
            + key_bias
        )
        top = jnp.max(logits, axis=1, keepdims=True)
        weights = jnp.exp(logits - top)
        total = jnp.sum(weights, axis=1, keepdims=True)
        weighted = jnp.sum(weights * value_grad, axis=1, keepdims=True)
        exp_ref[rows] = weights.reshape(CHUNK, PAD_HEADS, 128)
        grad_ref[rows] = value_grad.reshape(CHUNK, PAD_HEADS, 128)
        packed = jnp.where(lane == 0, top, jnp.where(lane == 1, total, jnp.where(lane == 2, weighted, 0.0)))
        packed = jnp.transpose(packed)
        for q in range(3):
            stats_ref[q * 8 + step : q * 8 + step + 1, :] = packed[q : q + 1]


def attention_parts(queries, near, far, pair_bias, pair_value, point_weight, mask_rows):
    part = jax.ShapeDtypeStruct(pair_bias.shape, jnp.float32)
    return pl.pallas_call(
        attention_kernel,
        in_specs=[SMEM] + [VMEM] * (5 + len(queries)),
        out_specs=[VMEM] * 3,
        out_shape=[part, part, jax.ShapeDtypeStruct((STATS, 128), jnp.float32)],
        scratch_shapes=[pltpu.VMEM((128, CAT), jnp.bfloat16), pltpu.VMEM((64, CAT), jnp.bfloat16)],
        compiler_params=PARAMS,
        cost_estimate=pl.CostEstimate(flops=4_000_000_000, bytes_accessed=2_000_000, transcendentals=200_000),
        name="attention_parts",
    )(point_weight, near, far, pair_bias, pair_value, mask_rows, *queries)


def bins_kernel(
    mask_smem, pair_ref, own_ref, labels_ref, near_ref, far_ref, bias_ref, mask_ref, bins_ref, weight_ref, mirror,
    mirror_labels,
):
    core = own_core()
    low_lanes = lax.broadcasted_iota(jnp.int32, (64, 128), 1) < 64

    def halves(slab):
        near = near_ref[slab].astype(jnp.int32).astype(jnp.float32)
        far = far_ref[slab].astype(jnp.int32).astype(jnp.float32)
        first = jnp.where(core == 0, near, far)
        second = jnp.where(core == 0, far, near)
        upper = jnp.where(low_lanes, first, pltpu.roll(second, 64, 1))
        lower = jnp.where(low_lanes, pltpu.roll(first, 64, 1), second)
        return upper, lower

    level, other_labels = halves(32)
    mirror_labels[...] = other_labels
    scale = jnp.exp2(level * (1.0 / 16.0)) * (1.0 / QUANT)

    def pair_of_bins(b, carry):
        upper, lower = halves(b)
        mirror[pl.ds(pl.multiple_of(b * 64, 64), 64), :] = upper * scale
        mirror[pl.ds(pl.multiple_of((b + 32) * 64, 64), 64), :] = lower * scale
        return carry

    lax.fori_loop(0, 32, pair_of_bins, 0, unroll=8)
    bias = jnp.sum(eye(64, jnp.float32) * bias_ref[...], axis=1, keepdims=True)
    bias = jnp.broadcast_to(bias, (64, 128))
    column_mask = mask_ref[pl.ds(lax.axis_index("col"), 1), :].astype(jnp.float32)
    bin_of = lax.broadcasted_iota(jnp.int32, (64, 128), 0)
    first_row = lax.axis_index("row") * 64

    total = jnp.zeros((64, 128), jnp.float32)
    for step in range(pair_ref.shape[0] // CHUNK):
        grads = []
        for t in range(CHUNK):
            row = step * CHUNK + t
            logits = own_ref[row] + mirror[pl.ds(row, 64, stride=64), :] + bias
            weights = jnp.exp(logits - jnp.max(logits, axis=0, keepdims=True))
            valid = column_mask * mask_smem[first_row + row].astype(jnp.float32)
            share = 2.0 * valid / jnp.sum(weights, axis=0, keepdims=True)
            own_label = labels_ref[pl.ds(row, 1), :]
            other_label = mirror_labels[pl.ds(row, 1), :].astype(jnp.int32)
            hits = jnp.where(bin_of == own_label, valid, 0.0) + jnp.where(bin_of == other_label, valid, 0.0)
            grad = (weights * share - hits).astype(jnp.bfloat16)
            bins_ref[row] = grad
            grads.append(grad)
        flat = pair_ref[step * CHUNK : (step + 1) * CHUNK].reshape(CHUNK * 128, 128)
        total += dot(jnp.concatenate(grads, axis=1), flat)
    weight_ref[...] = total


def bin_gradient(pair_tile, own, near, far, labels, dist_bias, mask_rows, residue_mask):
    rows = pair_tile.shape[0]
    return pl.pallas_call(
        bins_kernel,
        in_specs=[SMEM] + [VMEM] * 7,
        out_specs=[VMEM, VMEM],
        out_shape=[
            jax.ShapeDtypeStruct((rows, 64, 128), jnp.bfloat16),
            jax.ShapeDtypeStruct((64, 128), jnp.float32),
        ],
        scratch_shapes=[
            pltpu.VMEM((64 * 64, 128), jnp.float32),
            pltpu.VMEM((64, 128), jnp.float32),
        ],
        compiler_params=PARAMS,
        cost_estimate=pl.CostEstimate(flops=200_000_000, bytes_accessed=6_000_000, transcendentals=600_000),
        name="bin_gradient",
    )(residue_mask, pair_tile, own, labels, near, far, dist_bias, mask_rows)


def output_kernel(exp_ref, grad_ref, *refs):
    stats_refs, (bins_ref, cot_ref, weight_ref, bias_ref, out_hbm, out_ref, sent) = refs[:4], refs[4:]
    length = CHUNK * PAD_HEADS
    weight_t = weight_ref[...]
    bias_t = padded_heads(bias_ref)
    places = [(ref, BINS + STATS * y) for ref in stats_refs for y in (0, 1)]
    tops = [ref[at : at + 8, :] for ref, at in places]
    totals = [ref[at + 8 : at + 16, :] for ref, at in places]
    weighted = [ref[at + 16 : at + 24, :] for ref, at in places]
    top = functools.reduce(jnp.maximum, tops)
    factors = [jnp.exp(m - top) for m in tops]
    total = sum(f * s for f, s in zip(factors, totals))
    means = sum(f * s for f, s in zip(factors, weighted)) / total
    shares = factors[0] / total
    going = chunk_copies(out_ref, out_hbm, sent)
    for step in range(out_ref.shape[0] // CHUNK):
        share = jnp.transpose(jnp.broadcast_to(shares[step : step + 1], (length, 128)))
        mean = jnp.transpose(jnp.broadcast_to(means[step : step + 1], (length, 128)))
        rows = slice(step * CHUNK, (step + 1) * CHUNK)
        attention = exp_ref[rows].reshape(length, 128) * share
        logit_grad = attention * (grad_ref[rows].reshape(length, 128) - mean)
        attention = attention.astype(jnp.bfloat16)
        logit_grad = (logit_grad * LOGIT_WEIGHT).astype(jnp.bfloat16)
        for t in range(CHUNK):
            heads = slice(t * PAD_HEADS, (t + 1) * PAD_HEADS)
            row = step * CHUNK + t
            left = jnp.concatenate([bins_ref[row], attention[heads], logit_grad[heads]], axis=0)
            right = jnp.concatenate([weight_t, cot_ref[row], bias_t], axis=0)
            out_ref[row] = dot(left, right, TN).astype(jnp.bfloat16)
        going[step].start()
    for copy in going:
        copy.wait()


def pair_gradient(weights, value_grad, stats, bins, cot, weight_rows, bias_rows):
    rows = bins.shape[0]
    return pl.pallas_call(
        output_kernel,
        in_specs=[VMEM] * 10,
        out_specs=HBM,
        out_shape=jax.ShapeDtypeStruct((rows, 128, 128), jnp.bfloat16),
        scratch_shapes=[
            pltpu.VMEM((rows, 128, 128), jnp.bfloat16),
            pltpu.SemaphoreType.DMA((rows // CHUNK,)),
        ],
        compiler_params=PARAMS,
        cost_estimate=pl.CostEstimate(flops=300_000_000, bytes_accessed=5_000_000, transcendentals=10_000),
        name="pair_gradient",
    )(weights, value_grad, *stats, bins, cot, weight_rows, bias_rows)


def pack_kernel(stats_ref, own_ref, one_ref, two_ref, three_ref, out_ref):
    out_ref[:BINS] = (own_ref[...] + two_ref[...]) + (one_ref[...] + three_ref[...])
    out_ref[BINS:] = stats_ref[...]


def pack_more_kernel(own_ref, one_ref, two_ref, three_ref, out_ref):
    out_ref[:BINS] = (own_ref[:BINS] + two_ref[:BINS]) + (one_ref[:BINS] + three_ref[:BINS])
    out_ref[BINS : BINS + STATS] = own_ref[BINS:]
    out_ref[BINS + STATS :] = one_ref[BINS:]


def packed(kernel, rows, name, *arrays):
    return pl.pallas_call(
        kernel,
        in_specs=[VMEM] * len(arrays),
        out_specs=VMEM,
        out_shape=jax.ShapeDtypeStruct((rows, 128), jnp.float32),
        compiler_params=PARAMS,
        cost_estimate=pl.CostEstimate(flops=30_000, bytes_accessed=200_000, transcendentals=0),
        name=name,
    )(*arrays)


def trade(array, axis):
    return [array] + [lax.ppermute(array, AXES, trade_map(axis, d)) for d in (1, 2, 3)]


def body(
    pair_rep,
    labels,
    residue_mask,
    dist_weight,
    dist_bias,
    bias_weight,
    query_scalar,
    query_points,
    key_scalar,
    key_points,
    value_scalar,
    value_points,
    point_weight,
    cot_scalar,
    cot_points,
    cot_pair,
):
    mask_rows = residue_mask.reshape(8, 128)
    weight_rows = jnp.transpose(dist_weight)
    bias_rows = jnp.transpose(bias_weight)

    own, same, other, own_keys = own_logits(
        pair_rep, weight_rows, labels, (key_scalar, key_points, value_scalar, value_points)
    )
    same = lax.ppermute(same, AXES, FIRST_HOP)
    other = lax.ppermute(other, AXES, FIRST_HOP)
    near_keys = lax.ppermute(own_keys, AXES, MIRROR)
    same = lax.ppermute(same, AXES, SECOND_HOP[0])
    other = lax.ppermute(other, AXES, SECOND_HOP[1])
    pair_bias, pair_value, cot = pair_parts(pair_rep, cot_pair, bias_rows)
    same, pair_bias = lax.optimization_barrier((same, pair_bias))
    bins, term = bin_gradient(
        pair_rep, own, same, other, labels, dist_bias.reshape(1, 64), mask_rows, residue_mask
    )
    term = term + lax.ppermute(term, AXES, CORE_SWAP)
    near_keys, _ = lax.optimization_barrier((near_keys, term))
    far_keys = lax.ppermute(near_keys, AXES, CORE_SWAP)
    weights, value_grad, stats = attention_parts(
        (query_scalar, query_points, cot_scalar, cot_points),
        near_keys,
        far_keys,
        pair_bias,
        pair_value,
        point_weight,
        mask_rows,
    )
    message = packed(pack_kernel, BINS + STATS, "sum_z", stats, *trade(term, 2))
    message = packed(pack_more_kernel, BINS + 2 * STATS, "sum_y", *trade(message, 1))
    arrived = trade(message, 0)
    pair_grad = pair_gradient(weights, value_grad, arrived, bins, cot, weight_rows, bias_rows)
    own_sum, one, two, three = [a[:BINS] for a in arrived]
    return (pair_grad, jnp.transpose((own_sum + two) + (one + three)))


def solution(mesh):
    placed = (
        P("row", "col", None),
        P("row", "col"),
        P(),
        P(),
        P(),
        P(),
        P("row", None),
        P("row", None),
        P("row", None),
        P("row", None),
        P("row", None),
        P("row", None),
        P(),
        P("row", None),
        P("row", None),
        P("row", None),
    )
    return jax.shard_map(
        body, mesh=mesh, in_specs=placed, out_specs=(P("row", "col", None), P()), check_vma=False
    )
```

```python
import functools
import math

import jax
import jax.numpy as jnp
import numpy as np
from jax import lax
from jax.experimental import pallas as pl
from jax.experimental.pallas import tpu as pltpu
from jax.sharding import PartitionSpec as P

AXES = ("row", "col")
LOGIT_WEIGHT = math.sqrt(1.0 / 3.0)
HEADS = 12
PAD_HEADS = 16
CHUNK = 8
QUANT = 32760.0
BINS = 64
STATS = 24

WIDTHS = (192, 144, 192, 288)
PER_HEAD = (16, 12, 16, 24)
CAT = 896
WINDOWS = ((0, 256), (128, 384), (256, 896))
WINDOW_PARTS = ((0,), (1,), (2, 3))

NT = (((1,), (1,)), ((), ()))
TN = (((0,), (0,)), ((), ()))

CHIPS = [(x, y, z) for x in range(4) for y in range(4) for z in range(4)]
Y_SWAP = (0, 2, 1, 3)


def device_index(chip, core):
    x, y, z = chip
    return ((y // 2) * 8 + z * 2 + core) * 8 + (y % 2) * 4 + x


def mirror_chip(chip):
    x, y, z = chip
    return (z, Y_SWAP[y], x)


def halfway_chip(chip, core):
    x, y, z = chip
    if core == 0:
        return (x, y, (x + z) % 4)
    return ((x + 3 * z + 2) % 4, Y_SWAP[y], x)


FIRST_HOP = [(device_index(n, h), device_index(halfway_chip(n, h), h)) for n in CHIPS for h in (0, 1)]
SECOND_HOP = [
    [
        (device_index(halfway_chip(n, h), h), device_index(mirror_chip(n), (h + s) % 2))
        for n in CHIPS
        for h in (0, 1)
    ]
    for s in (0, 1)
]
CORE_SWAP = [(device_index(n, h), device_index(n, 1 - h)) for n in CHIPS for h in (0, 1)]


def trade_map(axis, bits):
    pairs = []
    for n in CHIPS:
        m = list(n)
        m[axis] ^= bits
        pairs += [(device_index(n, h), device_index(tuple(m), h)) for h in (0, 1)]
    return pairs


def head_columns(lo, hi, parts):
    head = lax.broadcasted_iota(jnp.int32, (PAD_HEADS, hi - lo), 0)
    column = lax.broadcasted_iota(jnp.int32, (PAD_HEADS, hi - lo), 1) + lo
    held = jnp.zeros((PAD_HEADS, hi - lo), jnp.float32)
    for part in parts:
        size = PER_HEAD[part]
        first = sum(WIDTHS[:part]) + head * size
        inside = (column >= first) & (column < first + size) & (head < HEADS)
        held = jnp.where(inside, 1.0, held)
    return held


def dot(a, b, dims=(((1,), (0,)), ((), ()))):
    return lax.dot_general(a, b, dims, preferred_element_type=jnp.float32)


def eye(n, dtype):
    return (
        lax.broadcasted_iota(jnp.int32, (n, n), 0) == lax.broadcasted_iota(jnp.int32, (n, n), 1)
    ).astype(dtype)


def padded_heads(bias_ref):
    heads = bias_ref.shape[0]
    pick = (
        lax.broadcasted_iota(jnp.int32, (PAD_HEADS, heads), 0)
        == lax.broadcasted_iota(jnp.int32, (PAD_HEADS, heads), 1)
    ).astype(jnp.bfloat16)
    return dot(pick, bias_ref[...]).astype(jnp.bfloat16)


def own_core():
    return lax.rem(lax.axis_index("row"), 2)


def lay_out(cat_ref, parts):
    start = 0
    for part in parts:
        width = part.shape[1]
        cat_ref[:, start : start + width] = part[...]
        start += width
    cat_ref[:, start:] = jnp.zeros((cat_ref.shape[0], cat_ref.shape[1] - start), cat_ref.dtype)


def chunk_copies(source, target, arrived):
    count = arrived.shape[0]
    size = source.shape[0] // count
    return [
        pltpu.make_async_copy(
            source.at[pl.ds(k * size, size)], target.at[pl.ds(k * size, size)], arrived.at[k]
        )
        for k in range(count)
    ]


HBM = pl.BlockSpec(memory_space=pltpu.HBM)
VMEM = pl.BlockSpec(memory_space=pltpu.VMEM)
SMEM = pl.BlockSpec(memory_space=pltpu.SMEM)
PARAMS = pltpu.CompilerParams(vmem_limit_bytes=16 * 1024 * 1024)


SLABS = 33
SLAB_PARTS = ((0, 8), (8, 16), (16, 24), (24, 33))


def logits_kernel(pair_hbm, weight_hbm, labels_hbm, *refs):
    keys_hbm, (own_hbm, same_hbm, other_hbm, cat_hbm) = refs[:4], refs[4:8]
    pair_ref, weight_ref, labels_ref, own_ref, same_ref, other_ref, cat_ref, slabs, top = refs[8:17]
    pair_sem, own_sem, slab_sem, small_sem = refs[17:21]
    keys_refs = refs[21:]
    copy = pltpu.make_async_copy
    weight_in = copy(weight_hbm, weight_ref, small_sem.at[0])
    small_in = [copy(labels_hbm, labels_ref, small_sem.at[1])]
    small_in += [copy(a, b, small_sem.at[3 + k]) for k, (a, b) in enumerate(zip(keys_hbm, keys_refs))]
    cat_out = copy(cat_ref, cat_hbm, small_sem.at[2])
    pair_in = chunk_copies(pair_hbm, pair_ref, pair_sem)
    own_out = chunk_copies(own_ref, own_hbm, own_sem)
    weight_in.start()
    for c in pair_in + small_in:
        c.start()
    weight_in.wait()
    weight_t = weight_ref[...]
    size = pair_ref.shape[0] // len(pair_in)
    for k in range(len(pair_in)):
        pair_in[k].wait()
        for first in range(k * size, (k + 1) * size, 4):
            flat = pair_ref[first : first + 4].reshape(4 * 128, 128)
            terms = dot(weight_t, flat, NT)
            for t in range(4):
                term = terms[:, t * 128 : (t + 1) * 128]
                row = first + t
                own_ref[row] = term
                slabs[pl.ds(row, 64, stride=64), :] = term
                top[pl.ds(row, 1), :] = jnp.max(jnp.abs(term), axis=0, keepdims=True)
        own_out[k].start()
    for c in small_in:
        c.wait()
    lay_out(cat_ref, keys_refs)
    cat_out.start()

    core = own_core()
    level = jnp.ceil(16.0 * jnp.log2(jnp.maximum(top[...], 1e-30)))
    scale = jnp.exp2(level * (-1.0 / 16.0)) * QUANT

    def narrow(values):
        return jnp.clip(jnp.round(values), -32767.0, 32767.0).astype(jnp.int32).astype(jnp.int16)

    def put(slab, upper, lower):
        turned = jnp.transpose(jnp.concatenate([upper, lower], axis=0))
        first, second = turned[:64], turned[64:]
        same_ref[slab] = narrow(jnp.where(core == 0, first, second))
        other_ref[slab] = narrow(jnp.where(core == 0, second, first))

    slab_out = []
    for part, (lo, hi) in enumerate(SLAB_PARTS):
        for b in range(lo, min(hi, 32)):
            put(b, slabs[b * 64 : (b + 1) * 64, :] * scale, slabs[(b + 32) * 64 : (b + 33) * 64, :] * scale)
        if hi == SLABS:
            put(32, level, labels_ref[...].astype(jnp.float32))
        for k, (ref, hbm) in enumerate(((same_ref, same_hbm), (other_ref, other_hbm))):
            slab_out.append(copy(ref.at[pl.ds(lo, hi - lo)], hbm.at[pl.ds(lo, hi - lo)], slab_sem.at[part, k]))
            slab_out[-1].start()
    for c in own_out + slab_out + [cat_out]:
        c.wait()


def own_logits(pair_tile, weight_rows, labels, keys):
    rows = pair_tile.shape[0]
    block = jax.ShapeDtypeStruct((SLABS, 64, 128), jnp.int16)
    cat = jax.ShapeDtypeStruct((rows, CAT), jnp.bfloat16)
    own = jax.ShapeDtypeStruct((rows, 64, 128), jnp.float32)
    arrays = [pair_tile, weight_rows, labels, own, block, block, cat]
    return pl.pallas_call(
        logits_kernel,
        in_specs=[HBM] * (3 + len(keys)),
        out_specs=[HBM] * 4,
        out_shape=[own, block, block, cat],
        scratch_shapes=[pltpu.VMEM(a.shape, a.dtype) for a in arrays]
        + [
            pltpu.VMEM((64 * 64, 128), jnp.float32),
            pltpu.VMEM((64, 128), jnp.float32),
            pltpu.SemaphoreType.DMA((8,)),
            pltpu.SemaphoreType.DMA((8,)),
            pltpu.SemaphoreType.DMA((len(SLAB_PARTS), 2)),
            pltpu.SemaphoreType.DMA((3 + len(keys),)),
        ]
        + [pltpu.VMEM(k.shape, k.dtype) for k in keys],
        compiler_params=pltpu.CompilerParams(vmem_limit_bytes=60 * 1024 * 1024),
        cost_estimate=pl.CostEstimate(flops=200_000_000, bytes_accessed=6_000_000, transcendentals=8192),
        name="own_logits",
    )(pair_tile, weight_rows, labels, *keys)


def pair_parts_kernel(pair_ref, cot_ref, bias_ref, bias_out_ref, value_out_ref, cot_out_ref, cot_rows):
    length = CHUNK * PAD_HEADS
    for h in range(HEADS):
        cot_rows[h * 64 : (h + 1) * 64] = cot_ref[:, h * 128 : (h + 1) * 128]
    bias_t = padded_heads(bias_ref)
    row_of = lax.broadcasted_iota(jnp.int32, (length, 768), 0)
    column_of = lax.broadcasted_iota(jnp.int32, (length, 768), 1)
    same_head = row_of % PAD_HEADS == column_of // 64
    place = column_of % 64 - row_of // PAD_HEADS
    for step in range(pair_ref.shape[0] // CHUNK):
        pick = (same_head & (place == step * CHUNK)).astype(jnp.bfloat16)
        cot = dot(pick, cot_rows[...]).astype(jnp.bfloat16)
        cot_out_ref[step * CHUNK : (step + 1) * CHUNK] = cot.reshape(CHUNK, PAD_HEADS, 128)
        for t in range(CHUNK):
            row = step * CHUNK + t
            both = jnp.concatenate([bias_t, cot[t * PAD_HEADS : (t + 1) * PAD_HEADS]], axis=0)
            result = dot(both, pair_ref[row], NT)
            bias_out_ref[row] = result[:PAD_HEADS]
            value_out_ref[row] = result[PAD_HEADS:]


def pair_parts(pair_tile, cot_pair, bias_rows):
    rows = pair_tile.shape[0]
    part = jax.ShapeDtypeStruct((rows, PAD_HEADS, 128), jnp.float32)
    return pl.pallas_call(
        pair_parts_kernel,
        in_specs=[VMEM] * 3,
        out_specs=[VMEM] * 3,
        out_shape=[part, part, jax.ShapeDtypeStruct((rows, PAD_HEADS, 128), jnp.bfloat16)],
        scratch_shapes=[pltpu.VMEM((768, 128), jnp.bfloat16)],
        compiler_params=PARAMS,
        cost_estimate=pl.CostEstimate(flops=1_000_000_000, bytes_accessed=4_000_000, transcendentals=0),
        name="pair_parts",
    )(pair_tile, cot_pair, bias_rows)


def attention_kernel(point_smem, near_ref, far_ref, pair_bias_ref, pair_value_ref, mask_ref, *refs):
    query_refs = refs[:4]
    exp_ref, grad_ref, stats_ref, keys, cat_ref = refs[4:]
    length = CHUNK * PAD_HEADS

    def iota(shape, dim):
        return lax.broadcasted_iota(jnp.int32, shape, dim)

    core = own_core()
    near, far = near_ref[...].astype(jnp.float32), far_ref[...].astype(jnp.float32)
    keys[:64] = jnp.where(core == 0, near, far).astype(jnp.bfloat16)
    keys[64:] = jnp.where(core == 0, far, near).astype(jnp.bfloat16)
    lay_out(cat_ref, query_refs)

    masks = [head_columns(lo, hi, parts) for (lo, hi), parts in zip(WINDOWS, WINDOW_PARTS)]
    right = [keys[:, lo:hi] for lo, hi in WINDOWS]
    key_points = right[1].astype(jnp.float32)
    key_sq = lax.dot_general(
        masks[1],
        key_points * key_points,
        NT,
        precision=lax.Precision.HIGHEST,
        preferred_element_type=jnp.float32,
    )
    key_sq = jnp.concatenate([key_sq] * CHUNK, axis=0)
    masks = [jnp.concatenate([mask] * CHUNK, axis=0) for mask in masks]

    head_of = iota((length, 128), 0) % PAD_HEADS
    raw = jnp.zeros((length, 128), jnp.float32)
    for h in range(HEADS):
        raw = jnp.where(head_of == h, point_smem[h], raw)
    softplus = jnp.maximum(raw, 0.0) + jnp.log1p(jnp.exp(-jnp.abs(raw)))
    point_scale = softplus * (math.sqrt(2.0 / 36.0) / 2.0)
    column_mask = mask_ref[pl.ds(lax.axis_index("col"), 1), :]
    key_bias = jnp.where(column_mask > 0, 0.0, -1000000000.0)
    lane = iota((length, 128), 1)
    place = iota((length, 64), 1) - iota((length, 64), 0) // PAD_HEADS

    for step in range(exp_ref.shape[0] // CHUNK):
        pick = (place == step * CHUNK).astype(jnp.bfloat16)
        spread = dot(pick, cat_ref[...])
        left = [spread[:, lo:hi] * mask for (lo, hi), mask in zip(WINDOWS, masks)]
        scalar_term, cross_term, value_term = [dot(a.astype(jnp.bfloat16), b, NT) for a, b in zip(left, right)]
        query_sq = jnp.sum(left[1] * left[1], axis=1, keepdims=True)
        rows = slice(step * CHUNK, (step + 1) * CHUNK)
        pair_bias = pair_bias_ref[rows].reshape(length, 128)
        value_grad = value_term + pair_value_ref[rows].reshape(length, 128)
        logits = (
            LOGIT_WEIGHT
            * (scalar_term * 0.25 + pair_bias - point_scale * (query_sq + key_sq - 2.0 * cross_term))
            + key_bias
        )
        top = jnp.max(logits, axis=1, keepdims=True)
        weights = jnp.exp(logits - top)
        total = jnp.sum(weights, axis=1, keepdims=True)
        weighted = jnp.sum(weights * value_grad, axis=1, keepdims=True)
        exp_ref[rows] = weights.reshape(CHUNK, PAD_HEADS, 128)
        grad_ref[rows] = value_grad.reshape(CHUNK, PAD_HEADS, 128)
        packed = jnp.where(lane == 0, top, jnp.where(lane == 1, total, jnp.where(lane == 2, weighted, 0.0)))
        packed = jnp.transpose(packed)
        for q in range(3):
            stats_ref[q * 8 + step : q * 8 + step + 1, :] = packed[q : q + 1]


def attention_parts(queries, near, far, pair_bias, pair_value, point_weight, mask_rows):
    part = jax.ShapeDtypeStruct(pair_bias.shape, jnp.float32)
    return pl.pallas_call(
        attention_kernel,
        in_specs=[SMEM] + [VMEM] * (5 + len(queries)),
        out_specs=[VMEM] * 3,
        out_shape=[part, part, jax.ShapeDtypeStruct((STATS, 128), jnp.float32)],
        scratch_shapes=[pltpu.VMEM((128, CAT), jnp.bfloat16), pltpu.VMEM((64, CAT), jnp.bfloat16)],
        compiler_params=PARAMS,
        cost_estimate=pl.CostEstimate(flops=4_000_000_000, bytes_accessed=2_000_000, transcendentals=200_000),
        name="attention_parts",
    )(point_weight, near, far, pair_bias, pair_value, mask_rows, *queries)


def bins_kernel(
    mask_smem, pair_ref, own_ref, labels_ref, near_ref, far_ref, bias_ref, mask_ref, bins_ref, weight_ref, mirror,
    mirror_labels,
):
    core = own_core()
    low_lanes = lax.broadcasted_iota(jnp.int32, (64, 128), 1) < 64

    def halves(slab):
        near = near_ref[slab].astype(jnp.int32).astype(jnp.float32)
        far = far_ref[slab].astype(jnp.int32).astype(jnp.float32)
        first = jnp.where(core == 0, near, far)
        second = jnp.where(core == 0, far, near)
        upper = jnp.where(low_lanes, first, pltpu.roll(second, 64, 1))
        lower = jnp.where(low_lanes, pltpu.roll(first, 64, 1), second)
        return upper, lower

    level, other_labels = halves(32)
    mirror_labels[...] = other_labels
    scale = jnp.exp2(level * (1.0 / 16.0)) * (1.0 / QUANT)

    def pair_of_bins(b, carry):
        upper, lower = halves(b)
        mirror[pl.ds(pl.multiple_of(b * 64, 64), 64), :] = upper * scale
        mirror[pl.ds(pl.multiple_of((b + 32) * 64, 64), 64), :] = lower * scale
        return carry

    lax.fori_loop(0, 32, pair_of_bins, 0, unroll=8)
    bias = jnp.sum(eye(64, jnp.float32) * bias_ref[...], axis=1, keepdims=True)
    bias = jnp.broadcast_to(bias, (64, 128))
    column_mask = mask_ref[pl.ds(lax.axis_index("col"), 1), :].astype(jnp.float32)
    bin_of = lax.broadcasted_iota(jnp.int32, (64, 128), 0)
    first_row = lax.axis_index("row") * 64

    total = jnp.zeros((64, 128), jnp.float32)
    for step in range(pair_ref.shape[0] // CHUNK):
        grads = []
        for t in range(CHUNK):
            row = step * CHUNK + t
            logits = own_ref[row] + mirror[pl.ds(row, 64, stride=64), :] + bias
            weights = jnp.exp(logits - jnp.max(logits, axis=0, keepdims=True))
            valid = column_mask * mask_smem[first_row + row].astype(jnp.float32)
            share = 2.0 * valid / jnp.sum(weights, axis=0, keepdims=True)
            own_label = labels_ref[pl.ds(row, 1), :]
            other_label = mirror_labels[pl.ds(row, 1), :].astype(jnp.int32)
            hits = jnp.where(bin_of == own_label, valid, 0.0) + jnp.where(bin_of == other_label, valid, 0.0)
            grad = (weights * share - hits).astype(jnp.bfloat16)
            bins_ref[row] = grad
            grads.append(grad)
        flat = pair_ref[step * CHUNK : (step + 1) * CHUNK].reshape(CHUNK * 128, 128)
        total += dot(jnp.concatenate(grads, axis=1), flat)
    weight_ref[...] = total


def bin_gradient(pair_tile, own, near, far, labels, dist_bias, mask_rows, residue_mask):
    rows = pair_tile.shape[0]
    return pl.pallas_call(
        bins_kernel,
        in_specs=[SMEM] + [VMEM] * 7,
        out_specs=[VMEM, VMEM],
        out_shape=[
            jax.ShapeDtypeStruct((rows, 64, 128), jnp.bfloat16),
            jax.ShapeDtypeStruct((64, 128), jnp.float32),
        ],
        scratch_shapes=[
            pltpu.VMEM((64 * 64, 128), jnp.float32),
            pltpu.VMEM((64, 128), jnp.float32),
        ],
        compiler_params=PARAMS,
        cost_estimate=pl.CostEstimate(flops=200_000_000, bytes_accessed=6_000_000, transcendentals=600_000),
        name="bin_gradient",
    )(residue_mask, pair_tile, own, labels, near, far, dist_bias, mask_rows)


def output_kernel(exp_ref, grad_ref, *refs):
    stats_refs, (bins_ref, cot_ref, weight_ref, bias_ref, out_hbm, sum_ref, out_ref, sent) = refs[:4], refs[4:]
    own_sum, one, two, three = [ref[:BINS] for ref in stats_refs]
    sum_ref[...] = (own_sum + two) + (one + three)
    length = CHUNK * PAD_HEADS
    weight_t = weight_ref[...]
    bias_t = padded_heads(bias_ref)
    places = [(ref, BINS + STATS * y) for ref in stats_refs for y in (0, 1)]
    tops = [ref[at : at + 8, :] for ref, at in places]
    totals = [ref[at + 8 : at + 16, :] for ref, at in places]
    weighted = [ref[at + 16 : at + 24, :] for ref, at in places]
    top = functools.reduce(jnp.maximum, tops)
    factors = [jnp.exp(m - top) for m in tops]
    total = sum(f * s for f, s in zip(factors, totals))
    means = sum(f * s for f, s in zip(factors, weighted)) / total
    shares = factors[0] / total
    going = chunk_copies(out_ref, out_hbm, sent)
    for step in range(out_ref.shape[0] // CHUNK):
        share = jnp.transpose(jnp.broadcast_to(shares[step : step + 1], (length, 128)))
        mean = jnp.transpose(jnp.broadcast_to(means[step : step + 1], (length, 128)))
        rows = slice(step * CHUNK, (step + 1) * CHUNK)
        attention = exp_ref[rows].reshape(length, 128) * share
        logit_grad = attention * (grad_ref[rows].reshape(length, 128) - mean)
        attention = attention.astype(jnp.bfloat16)
        logit_grad = (logit_grad * LOGIT_WEIGHT).astype(jnp.bfloat16)
        for t in range(CHUNK):
            heads = slice(t * PAD_HEADS, (t + 1) * PAD_HEADS)
            row = step * CHUNK + t
            left = jnp.concatenate([bins_ref[row], attention[heads], logit_grad[heads]], axis=0)
            right = jnp.concatenate([weight_t, cot_ref[row], bias_t], axis=0)
            out_ref[row] = dot(left, right, TN).astype(jnp.bfloat16)
        going[step].start()
    for copy in going:
        copy.wait()


def pair_gradient(weights, value_grad, stats, bins, cot, weight_rows, bias_rows):
    rows = bins.shape[0]
    return pl.pallas_call(
        output_kernel,
        in_specs=[VMEM] * 10,
        out_specs=[HBM, VMEM],
        out_shape=[
            jax.ShapeDtypeStruct((rows, 128, 128), jnp.bfloat16),
            jax.ShapeDtypeStruct((BINS, 128), jnp.float32),
        ],
        scratch_shapes=[
            pltpu.VMEM((rows, 128, 128), jnp.bfloat16),
            pltpu.SemaphoreType.DMA((rows // CHUNK,)),
        ],
        compiler_params=PARAMS,
        cost_estimate=pl.CostEstimate(flops=300_000_000, bytes_accessed=5_000_000, transcendentals=10_000),
        name="pair_gradient",
    )(weights, value_grad, *stats, bins, cot, weight_rows, bias_rows)


def pack_kernel(stats_ref, own_ref, one_ref, two_ref, three_ref, out_ref):
    out_ref[:BINS] = (own_ref[...] + two_ref[...]) + (one_ref[...] + three_ref[...])
    out_ref[BINS:] = stats_ref[...]


def pack_more_kernel(own_ref, one_ref, two_ref, three_ref, out_ref):
    out_ref[:BINS] = (own_ref[:BINS] + two_ref[:BINS]) + (one_ref[:BINS] + three_ref[:BINS])
    out_ref[BINS : BINS + STATS] = own_ref[BINS:]
    out_ref[BINS + STATS :] = one_ref[BINS:]


def packed(kernel, rows, name, *arrays):
    return pl.pallas_call(
        kernel,
        in_specs=[VMEM] * len(arrays),
        out_specs=VMEM,
        out_shape=jax.ShapeDtypeStruct((rows, 128), jnp.float32),
        compiler_params=PARAMS,
        cost_estimate=pl.CostEstimate(flops=30_000, bytes_accessed=200_000, transcendentals=0),
        name=name,
    )(*arrays)


def trade(array, axis):
    return [array] + [lax.ppermute(array, AXES, trade_map(axis, d)) for d in (1, 2, 3)]


def body(
    pair_rep,
    labels,
    residue_mask,
    dist_weight,
    dist_bias,
    bias_weight,
    query_scalar,
    query_points,
    key_scalar,
    key_points,
    value_scalar,
    value_points,
    point_weight,
    cot_scalar,
    cot_points,
    cot_pair,
):
    mask_rows = residue_mask.reshape(8, 128)
    weight_rows = jnp.transpose(dist_weight)
    bias_rows = jnp.transpose(bias_weight)

    own, same, other, own_keys = own_logits(
        pair_rep, weight_rows, labels, (key_scalar, key_points, value_scalar, value_points)
    )
    same = lax.ppermute(same, AXES, FIRST_HOP)
    other = lax.ppermute(other, AXES, FIRST_HOP)
    near_keys = lax.ppermute(own_keys, AXES, FIRST_HOP)
    other, near_keys = lax.optimization_barrier((other, near_keys))
    bias_rows, _ = lax.optimization_barrier((bias_rows, other))
    pair_bias, pair_value, cot = pair_parts(pair_rep, cot_pair, bias_rows)
    same = lax.ppermute(same, AXES, SECOND_HOP[0])
    other = lax.ppermute(other, AXES, SECOND_HOP[1])
    near_keys = lax.ppermute(near_keys, AXES, SECOND_HOP[0])
    same, pair_bias = lax.optimization_barrier((same, pair_bias))
    bins, term = bin_gradient(
        pair_rep, own, same, other, labels, dist_bias.reshape(1, 64), mask_rows, residue_mask
    )
    term = term + lax.ppermute(term, AXES, CORE_SWAP)
    near_keys, _ = lax.optimization_barrier((near_keys, term))
    far_keys = lax.ppermute(near_keys, AXES, CORE_SWAP)
    weights, value_grad, stats = attention_parts(
        (query_scalar, query_points, cot_scalar, cot_points),
        near_keys,
        far_keys,
        pair_bias,
        pair_value,
        point_weight,
        mask_rows,
    )
    message = packed(pack_kernel, BINS + STATS, "sum_z", stats, *trade(term, 2))
    message = packed(pack_more_kernel, BINS + 2 * STATS, "sum_y", *trade(message, 1))
    arrived = trade(message, 0)
    pair_grad, weight_sum = pair_gradient(weights, value_grad, arrived, bins, cot, weight_rows, bias_rows)
    return (pair_grad, jnp.transpose(weight_sum))


def solution(mesh):
    placed = (
        P("row", "col", None),
        P("row", "col"),
        P(),
        P(),
        P(),
        P(),
        P("row", None),
        P("row", None),
        P("row", None),
        P("row", None),
        P("row", None),
        P("row", None),
        P(),
        P("row", None),
        P("row", None),
        P("row", None),
    )
    return jax.shard_map(
        body, mesh=mesh, in_specs=placed, out_specs=(P("row", "col", None), P()), check_vma=False
    )
```

```python
import functools
import math

import jax
import jax.numpy as jnp
import numpy as np
from jax import lax
from jax.experimental import pallas as pl
from jax.experimental.pallas import tpu as pltpu
from jax.sharding import PartitionSpec as P

AXES = ("row", "col")
LOGIT_WEIGHT = math.sqrt(1.0 / 3.0)
HEADS = 12
PAD_HEADS = 16
CHUNK = 8
QUANT = 32760.0
BINS = 64
STATS = 24

WIDTHS = (192, 144, 192, 288)
PER_HEAD = (16, 12, 16, 24)
CAT = 896
WINDOWS = ((0, 256), (128, 384), (256, 896))
WINDOW_PARTS = ((0,), (1,), (2, 3))

NT = (((1,), (1,)), ((), ()))
TN = (((0,), (0,)), ((), ()))

CHIPS = [(x, y, z) for x in range(4) for y in range(4) for z in range(4)]
Y_SWAP = (0, 2, 1, 3)


def device_index(chip, core):
    x, y, z = chip
    return ((y // 2) * 8 + z * 2 + core) * 8 + (y % 2) * 4 + x


def mirror_chip(chip):
    x, y, z = chip
    return (z, Y_SWAP[y], x)


def halfway_chip(chip, core):
    x, y, z = chip
    if core == 0:
        return (x, y, (x + z) % 4)
    return ((x + 3 * z + 2) % 4, Y_SWAP[y], x)


FIRST_HOP = [(device_index(n, h), device_index(halfway_chip(n, h), h)) for n in CHIPS for h in (0, 1)]
SECOND_HOP = [
    [
        (device_index(halfway_chip(n, h), h), device_index(mirror_chip(n), (h + s) % 2))
        for n in CHIPS
        for h in (0, 1)
    ]
    for s in (0, 1)
]
CORE_SWAP = [(device_index(n, h), device_index(n, 1 - h)) for n in CHIPS for h in (0, 1)]


def trade_map(axis, bits):
    pairs = []
    for n in CHIPS:
        m = list(n)
        m[axis] ^= bits
        pairs += [(device_index(n, h), device_index(tuple(m), h)) for h in (0, 1)]
    return pairs


def head_columns(lo, hi, parts):
    head = lax.broadcasted_iota(jnp.int32, (PAD_HEADS, hi - lo), 0)
    column = lax.broadcasted_iota(jnp.int32, (PAD_HEADS, hi - lo), 1) + lo
    held = jnp.zeros((PAD_HEADS, hi - lo), jnp.float32)
    for part in parts:
        size = PER_HEAD[part]
        first = sum(WIDTHS[:part]) + head * size
        inside = (column >= first) & (column < first + size) & (head < HEADS)
        held = jnp.where(inside, 1.0, held)
    return held


def dot(a, b, dims=(((1,), (0,)), ((), ()))):
    return lax.dot_general(a, b, dims, preferred_element_type=jnp.float32)


def eye(n, dtype):
    return (
        lax.broadcasted_iota(jnp.int32, (n, n), 0) == lax.broadcasted_iota(jnp.int32, (n, n), 1)
    ).astype(dtype)


def padded_heads(bias_ref):
    heads = bias_ref.shape[0]
    pick = (
        lax.broadcasted_iota(jnp.int32, (PAD_HEADS, heads), 0)
        == lax.broadcasted_iota(jnp.int32, (PAD_HEADS, heads), 1)
    ).astype(jnp.bfloat16)
    return dot(pick, bias_ref[...]).astype(jnp.bfloat16)


def own_core():
    return lax.rem(lax.axis_index("row"), 2)


def lay_out(cat_ref, parts):
    start = 0
    for part in parts:
        width = part.shape[1]
        cat_ref[:, start : start + width] = part[...]
        start += width
    cat_ref[:, start:] = jnp.zeros((cat_ref.shape[0], cat_ref.shape[1] - start), cat_ref.dtype)


def chunk_copies(source, target, arrived):
    count = arrived.shape[0]
    size = source.shape[0] // count
    return [
        pltpu.make_async_copy(
            source.at[pl.ds(k * size, size)], target.at[pl.ds(k * size, size)], arrived.at[k]
        )
        for k in range(count)
    ]


HBM = pl.BlockSpec(memory_space=pltpu.HBM)
VMEM = pl.BlockSpec(memory_space=pltpu.VMEM)
SMEM = pl.BlockSpec(memory_space=pltpu.SMEM)
PARAMS = pltpu.CompilerParams(vmem_limit_bytes=16 * 1024 * 1024)


SLABS = 33
KEY_SLABS = CAT // 128
SLAB_PARTS = ((0, 8), (8, 16), (16, 24), (24, 33))


def logits_kernel(pair_hbm, weight_hbm, labels_hbm, *refs):
    keys_hbm, (own_hbm, same_hbm, other_hbm) = refs[:4], refs[4:7]
    pair_ref, weight_ref, labels_ref, own_ref, same_ref, other_ref, cat_ref, slabs, top = refs[7:16]
    pair_sem, own_sem, slab_sem, small_sem = refs[16:20]
    keys_refs = refs[20:]
    copy = pltpu.make_async_copy
    weight_in = copy(weight_hbm, weight_ref, small_sem.at[0])
    small_in = [copy(labels_hbm, labels_ref, small_sem.at[1])]
    small_in += [copy(a, b, small_sem.at[3 + k]) for k, (a, b) in enumerate(zip(keys_hbm, keys_refs))]
    keys_out = copy(same_ref.at[pl.ds(SLABS, KEY_SLABS)], same_hbm.at[pl.ds(SLABS, KEY_SLABS)], small_sem.at[2])
    pair_in = chunk_copies(pair_hbm, pair_ref, pair_sem)
    own_out = chunk_copies(own_ref, own_hbm, own_sem)
    weight_in.start()
    for c in pair_in + small_in:
        c.start()
    weight_in.wait()
    weight_t = weight_ref[...]
    size = pair_ref.shape[0] // len(pair_in)
    for k in range(len(pair_in)):
        pair_in[k].wait()
        for first in range(k * size, (k + 1) * size, 4):
            flat = pair_ref[first : first + 4].reshape(4 * 128, 128)
            terms = dot(weight_t, flat, NT)
            for t in range(4):
                term = terms[:, t * 128 : (t + 1) * 128]
                row = first + t
                own_ref[row] = term
                slabs[pl.ds(row, 64, stride=64), :] = term
                top[pl.ds(row, 1), :] = jnp.max(jnp.abs(term), axis=0, keepdims=True)
        own_out[k].start()
    for c in small_in:
        c.wait()
    lay_out(cat_ref, keys_refs)

    def narrow(values):
        return jnp.clip(jnp.round(values), -32767.0, 32767.0).astype(jnp.int32).astype(jnp.int16)

    cat = cat_ref[...].astype(jnp.float32)
    column = lax.broadcasted_iota(jnp.int32, cat.shape, 1)
    coded = jnp.zeros_like(cat)
    for part, width in enumerate(WIDTHS):
        start = sum(WIDTHS[:part])
        held = (column >= start) & (column < start + width)
        largest = jnp.max(jnp.where(held, jnp.abs(cat), 0.0), axis=1, keepdims=True)
        part_level = jnp.ceil(16.0 * jnp.log2(jnp.maximum(largest, 1e-30)))
        coded = jnp.where(held, cat * (jnp.exp2(part_level * (-1.0 / 16.0)) * QUANT), coded)
        coded = jnp.where(column == sum(WIDTHS) + part, part_level, coded)
    coded = narrow(coded)
    for k in range(KEY_SLABS):
        same_ref[SLABS + k] = coded[:, k * 128 : (k + 1) * 128]
    keys_out.start()

    core = own_core()
    level = jnp.ceil(16.0 * jnp.log2(jnp.maximum(top[...], 1e-30)))
    scale = jnp.exp2(level * (-1.0 / 16.0)) * QUANT

    def put(slab, upper, lower):
        turned = jnp.transpose(jnp.concatenate([upper, lower], axis=0))
        first, second = turned[:64], turned[64:]
        same_ref[slab] = narrow(jnp.where(core == 0, first, second))
        other_ref[slab] = narrow(jnp.where(core == 0, second, first))

    slab_out = []
    for part, (lo, hi) in enumerate(SLAB_PARTS):
        for b in range(lo, min(hi, 32)):
            put(b, slabs[b * 64 : (b + 1) * 64, :] * scale, slabs[(b + 32) * 64 : (b + 33) * 64, :] * scale)
        if hi == SLABS:
            put(32, level, labels_ref[...].astype(jnp.float32))
        for k, (ref, hbm) in enumerate(((same_ref, same_hbm), (other_ref, other_hbm))):
            slab_out.append(copy(ref.at[pl.ds(lo, hi - lo)], hbm.at[pl.ds(lo, hi - lo)], slab_sem.at[part, k]))
            slab_out[-1].start()
    for c in own_out + slab_out + [keys_out]:
        c.wait()


def own_logits(pair_tile, weight_rows, labels, keys):
    rows = pair_tile.shape[0]
    same = jax.ShapeDtypeStruct((SLABS + KEY_SLABS, 64, 128), jnp.int16)
    other = jax.ShapeDtypeStruct((SLABS, 64, 128), jnp.int16)
    cat = jax.ShapeDtypeStruct((rows, CAT), jnp.bfloat16)
    own = jax.ShapeDtypeStruct((rows, 64, 128), jnp.float32)
    arrays = [pair_tile, weight_rows, labels, own, same, other, cat]
    return pl.pallas_call(
        logits_kernel,
        in_specs=[HBM] * (3 + len(keys)),
        out_specs=[HBM] * 3,
        out_shape=[own, same, other],
        scratch_shapes=[pltpu.VMEM(a.shape, a.dtype) for a in arrays]
        + [
            pltpu.VMEM((64 * 64, 128), jnp.float32),
            pltpu.VMEM((64, 128), jnp.float32),
            pltpu.SemaphoreType.DMA((8,)),
            pltpu.SemaphoreType.DMA((8,)),
            pltpu.SemaphoreType.DMA((len(SLAB_PARTS), 2)),
            pltpu.SemaphoreType.DMA((3 + len(keys),)),
        ]
        + [pltpu.VMEM(k.shape, k.dtype) for k in keys],
        compiler_params=pltpu.CompilerParams(vmem_limit_bytes=60 * 1024 * 1024),
        cost_estimate=pl.CostEstimate(flops=200_000_000, bytes_accessed=6_000_000, transcendentals=8192),
        name="own_logits",
    )(pair_tile, weight_rows, labels, *keys)


def pair_parts_kernel(pair_ref, cot_ref, bias_ref, bias_out_ref, value_out_ref, cot_out_ref, cot_rows):
    length = CHUNK * PAD_HEADS
    for h in range(HEADS):
        cot_rows[h * 64 : (h + 1) * 64] = cot_ref[:, h * 128 : (h + 1) * 128]
    bias_t = padded_heads(bias_ref)
    row_of = lax.broadcasted_iota(jnp.int32, (length, 768), 0)
    column_of = lax.broadcasted_iota(jnp.int32, (length, 768), 1)
    same_head = row_of % PAD_HEADS == column_of // 64
    place = column_of % 64 - row_of // PAD_HEADS
    for step in range(pair_ref.shape[0] // CHUNK):
        pick = (same_head & (place == step * CHUNK)).astype(jnp.bfloat16)
        cot = dot(pick, cot_rows[...]).astype(jnp.bfloat16)
        cot_out_ref[step * CHUNK : (step + 1) * CHUNK] = cot.reshape(CHUNK, PAD_HEADS, 128)
        for t in range(CHUNK):
            row = step * CHUNK + t
            both = jnp.concatenate([bias_t, cot[t * PAD_HEADS : (t + 1) * PAD_HEADS]], axis=0)
            result = dot(both, pair_ref[row], NT)
            bias_out_ref[row] = result[:PAD_HEADS]
            value_out_ref[row] = result[PAD_HEADS:]


def pair_parts(pair_tile, cot_pair, bias_rows):
    rows = pair_tile.shape[0]
    part = jax.ShapeDtypeStruct((rows, PAD_HEADS, 128), jnp.float32)
    return pl.pallas_call(
        pair_parts_kernel,
        in_specs=[VMEM] * 3,
        out_specs=[VMEM] * 3,
        out_shape=[part, part, jax.ShapeDtypeStruct((rows, PAD_HEADS, 128), jnp.bfloat16)],
        scratch_shapes=[pltpu.VMEM((768, 128), jnp.bfloat16)],
        compiler_params=PARAMS,
        cost_estimate=pl.CostEstimate(flops=300_000_000, bytes_accessed=4_000_000, transcendentals=0),
        name="pair_parts",
    )(pair_tile, cot_pair, bias_rows)


def attention_kernel(point_smem, near_ref, far_ref, pair_bias_ref, pair_value_ref, mask_ref, *refs):
    query_refs = refs[:4]
    exp_ref, grad_ref, stats_ref, keys, cat_ref = refs[4:]
    length = CHUNK * PAD_HEADS

    def iota(shape, dim):
        return lax.broadcasted_iota(jnp.int32, shape, dim)

    core = own_core()

    def decoded(ref, first):
        coded = jnp.concatenate(
            [ref[first + k].astype(jnp.int32).astype(jnp.float32) for k in range(KEY_SLABS)], axis=1
        )
        column = iota(coded.shape, 1)
        scale = jnp.zeros_like(coded)
        for part, width in enumerate(WIDTHS):
            start = sum(WIDTHS[:part])
            at = sum(WIDTHS) + part
            part_scale = jnp.exp2(coded[:, at : at + 1] * (1.0 / 16.0)) * (1.0 / QUANT)
            scale = jnp.where((column >= start) & (column < start + width), part_scale, scale)
        return coded * scale

    near, far = decoded(near_ref, SLABS), decoded(far_ref, 0)
    keys[:64] = jnp.where(core == 0, near, far).astype(jnp.bfloat16)
    keys[64:] = jnp.where(core == 0, far, near).astype(jnp.bfloat16)
    lay_out(cat_ref, query_refs)

    masks = [head_columns(lo, hi, parts) for (lo, hi), parts in zip(WINDOWS, WINDOW_PARTS)]
    right = [keys[:, lo:hi] for lo, hi in WINDOWS]
    key_points = right[1].astype(jnp.float32)
    key_sq = lax.dot_general(
        masks[1],
        key_points * key_points,
        NT,
        precision=lax.Precision.HIGHEST,
        preferred_element_type=jnp.float32,
    )
    key_sq = jnp.concatenate([key_sq] * CHUNK, axis=0)
    masks = [jnp.concatenate([mask] * CHUNK, axis=0) for mask in masks]

    head_of = iota((length, 128), 0) % PAD_HEADS
    raw = jnp.zeros((length, 128), jnp.float32)
    for h in range(HEADS):
        raw = jnp.where(head_of == h, point_smem[h], raw)
    softplus = jnp.maximum(raw, 0.0) + jnp.log1p(jnp.exp(-jnp.abs(raw)))
    point_scale = softplus * (math.sqrt(2.0 / 36.0) / 2.0)
    column_mask = mask_ref[pl.ds(lax.axis_index("col"), 1), :]
    key_bias = jnp.where(column_mask > 0, 0.0, -1000000000.0)
    lane = iota((length, 128), 1)
    place = iota((length, 64), 1) - iota((length, 64), 0) // PAD_HEADS

    for step in range(exp_ref.shape[0] // CHUNK):
        pick = (place == step * CHUNK).astype(jnp.bfloat16)
        spread = dot(pick, cat_ref[...])
        left = [spread[:, lo:hi] * mask for (lo, hi), mask in zip(WINDOWS, masks)]
        scalar_term, cross_term, value_term = [dot(a.astype(jnp.bfloat16), b, NT) for a, b in zip(left, right)]
        query_sq = jnp.sum(left[1] * left[1], axis=1, keepdims=True)
        rows = slice(step * CHUNK, (step + 1) * CHUNK)
        pair_bias = pair_bias_ref[rows].reshape(length, 128)
        value_grad = value_term + pair_value_ref[rows].reshape(length, 128)
        logits = (
            LOGIT_WEIGHT
            * (scalar_term * 0.25 + pair_bias - point_scale * (query_sq + key_sq - 2.0 * cross_term))
            + key_bias
        )
        top = jnp.max(logits, axis=1, keepdims=True)
        weights = jnp.exp(logits - top)
        total = jnp.sum(weights, axis=1, keepdims=True)
        weighted = jnp.sum(weights * value_grad, axis=1, keepdims=True)
        exp_ref[rows] = weights.reshape(CHUNK, PAD_HEADS, 128)
        grad_ref[rows] = value_grad.reshape(CHUNK, PAD_HEADS, 128)
        packed = jnp.where(lane == 0, top, jnp.where(lane == 1, total, jnp.where(lane == 2, weighted, 0.0)))
        packed = jnp.transpose(packed)
        for q in range(3):
            stats_ref[q * 8 + step : q * 8 + step + 1, :] = packed[q : q + 1]


def attention_parts(queries, near, far, pair_bias, pair_value, point_weight, mask_rows):
    part = jax.ShapeDtypeStruct(pair_bias.shape, jnp.float32)
    return pl.pallas_call(
        attention_kernel,
        in_specs=[SMEM] + [VMEM] * (5 + len(queries)),
        out_specs=[VMEM] * 3,
        out_shape=[part, part, jax.ShapeDtypeStruct((STATS, 128), jnp.float32)],
        scratch_shapes=[pltpu.VMEM((128, CAT), jnp.bfloat16), pltpu.VMEM((64, CAT), jnp.bfloat16)],
        compiler_params=PARAMS,
        cost_estimate=pl.CostEstimate(flops=500_000_000, bytes_accessed=2_000_000, transcendentals=200_000),
        name="attention_parts",
    )(point_weight, near, far, pair_bias, pair_value, mask_rows, *queries)


def bins_kernel(
    mask_smem, pair_ref, own_ref, labels_ref, near_ref, far_ref, bias_ref, mask_ref, bins_ref, weight_ref, mirror,
    mirror_labels,
):
    core = own_core()
    low_lanes = lax.broadcasted_iota(jnp.int32, (64, 128), 1) < 64

    def halves(slab):
        near = near_ref[slab].astype(jnp.int32).astype(jnp.float32)
        far = far_ref[slab].astype(jnp.int32).astype(jnp.float32)
        first = jnp.where(core == 0, near, far)
        second = jnp.where(core == 0, far, near)
        upper = jnp.where(low_lanes, first, pltpu.roll(second, 64, 1))
        lower = jnp.where(low_lanes, pltpu.roll(first, 64, 1), second)
        return upper, lower

    level, other_labels = halves(32)
    mirror_labels[...] = other_labels
    scale = jnp.exp2(level * (1.0 / 16.0)) * (1.0 / QUANT)

    def pair_of_bins(b, carry):
        upper, lower = halves(b)
        mirror[pl.ds(pl.multiple_of(b * 64, 64), 64), :] = upper * scale
        mirror[pl.ds(pl.multiple_of((b + 32) * 64, 64), 64), :] = lower * scale
        return carry

    lax.fori_loop(0, 32, pair_of_bins, 0, unroll=8)
    bias = jnp.sum(eye(64, jnp.float32) * bias_ref[...], axis=1, keepdims=True)
    bias = jnp.broadcast_to(bias, (64, 128))
    column_mask = mask_ref[pl.ds(lax.axis_index("col"), 1), :].astype(jnp.float32)
    bin_of = lax.broadcasted_iota(jnp.int32, (64, 128), 0)
    first_row = lax.axis_index("row") * 64

    total = jnp.zeros((64, 128), jnp.float32)
    for step in range(pair_ref.shape[0] // CHUNK):
        grads = []
        for t in range(CHUNK):
            row = step * CHUNK + t
            logits = own_ref[row] + mirror[pl.ds(row, 64, stride=64), :] + bias
            weights = jnp.exp(logits - jnp.max(logits, axis=0, keepdims=True))
            valid = column_mask * mask_smem[first_row + row].astype(jnp.float32)
            share = 2.0 * valid / jnp.sum(weights, axis=0, keepdims=True)
            own_label = labels_ref[pl.ds(row, 1), :]
            other_label = mirror_labels[pl.ds(row, 1), :].astype(jnp.int32)
            hits = jnp.where(bin_of == own_label, valid, 0.0) + jnp.where(bin_of == other_label, valid, 0.0)
            grad = (weights * share - hits).astype(jnp.bfloat16)
            bins_ref[row] = grad
            grads.append(grad)
        flat = pair_ref[step * CHUNK : (step + 1) * CHUNK].reshape(CHUNK * 128, 128)
        total += dot(jnp.concatenate(grads, axis=1), flat)
    weight_ref[...] = total


def bin_gradient(pair_tile, own, near, far, labels, dist_bias, mask_rows, residue_mask):
    rows = pair_tile.shape[0]
    return pl.pallas_call(
        bins_kernel,
        in_specs=[SMEM] + [VMEM] * 7,
        out_specs=[VMEM, VMEM],
        out_shape=[
            jax.ShapeDtypeStruct((rows, 64, 128), jnp.bfloat16),
            jax.ShapeDtypeStruct((64, 128), jnp.float32),
        ],
        scratch_shapes=[
            pltpu.VMEM((64 * 64, 128), jnp.float32),
            pltpu.VMEM((64, 128), jnp.float32),
        ],
        compiler_params=PARAMS,
        cost_estimate=pl.CostEstimate(flops=200_000_000, bytes_accessed=6_000_000, transcendentals=600_000),
        name="bin_gradient",
    )(residue_mask, pair_tile, own, labels, near, far, dist_bias, mask_rows)


def output_kernel(exp_ref, grad_ref, *refs):
    stats_refs, (bins_ref, cot_ref, weight_ref, bias_ref, out_hbm, out_ref, sent) = refs[:4], refs[4:]
    length = CHUNK * PAD_HEADS
    weight_t = weight_ref[...]
    bias_t = padded_heads(bias_ref)
    places = [(ref, BINS + STATS * y) for ref in stats_refs for y in (0, 1)]
    tops = [ref[at : at + 8, :] for ref, at in places]
    totals = [ref[at + 8 : at + 16, :] for ref, at in places]
    weighted = [ref[at + 16 : at + 24, :] for ref, at in places]
    top = functools.reduce(jnp.maximum, tops)
    factors = [jnp.exp(m - top) for m in tops]
    total = sum(f * s for f, s in zip(factors, totals))
    means = sum(f * s for f, s in zip(factors, weighted)) / total
    shares = factors[0] / total
    going = chunk_copies(out_ref, out_hbm, sent)
    for step in range(out_ref.shape[0] // CHUNK):
        share = jnp.transpose(jnp.broadcast_to(shares[step : step + 1], (length, 128)))
        mean = jnp.transpose(jnp.broadcast_to(means[step : step + 1], (length, 128)))
        rows = slice(step * CHUNK, (step + 1) * CHUNK)
        attention = exp_ref[rows].reshape(length, 128) * share
        logit_grad = attention * (grad_ref[rows].reshape(length, 128) - mean)
        attention = attention.astype(jnp.bfloat16)
        logit_grad = (logit_grad * LOGIT_WEIGHT).astype(jnp.bfloat16)
        for t in range(CHUNK):
            heads = slice(t * PAD_HEADS, (t + 1) * PAD_HEADS)
            row = step * CHUNK + t
            left = jnp.concatenate([bins_ref[row], attention[heads], logit_grad[heads]], axis=0)
            right = jnp.concatenate([weight_t, cot_ref[row], bias_t], axis=0)
            out_ref[row] = dot(left, right, TN).astype(jnp.bfloat16)
        going[step].start()
    for copy in going:
        copy.wait()


def pair_gradient(weights, value_grad, stats, bins, cot, weight_rows, bias_rows):
    rows = bins.shape[0]
    return pl.pallas_call(
        output_kernel,
        in_specs=[VMEM] * 10,
        out_specs=HBM,
        out_shape=jax.ShapeDtypeStruct((rows, 128, 128), jnp.bfloat16),
        scratch_shapes=[
            pltpu.VMEM((rows, 128, 128), jnp.bfloat16),
            pltpu.SemaphoreType.DMA((rows // CHUNK,)),
        ],
        compiler_params=PARAMS,
        cost_estimate=pl.CostEstimate(flops=300_000_000, bytes_accessed=5_000_000, transcendentals=10_000),
        name="pair_gradient",
    )(weights, value_grad, *stats, bins, cot, weight_rows, bias_rows)


def pack_kernel(term_ref, swapped_ref, stats_ref, out_ref):
    out_ref[:BINS] = term_ref[...] + swapped_ref[...]
    out_ref[BINS:] = stats_ref[...]


def pack_more_kernel(own_ref, one_ref, two_ref, three_ref, out_ref):
    out_ref[:BINS] = (own_ref[:BINS] + two_ref[:BINS]) + (one_ref[:BINS] + three_ref[:BINS])
    if out_ref.shape[0] > BINS:
        out_ref[BINS : BINS + STATS] = own_ref[BINS:]
        out_ref[BINS + STATS :] = one_ref[BINS:]


def packed(kernel, rows, name, *arrays):
    return pl.pallas_call(
        kernel,
        in_specs=[VMEM] * len(arrays),
        out_specs=VMEM,
        out_shape=jax.ShapeDtypeStruct((rows, 128), jnp.float32),
        compiler_params=PARAMS,
        cost_estimate=pl.CostEstimate(flops=30_000, bytes_accessed=200_000, transcendentals=0),
        name=name,
    )(*arrays)


def trade(array, axis):
    return [array] + [lax.ppermute(array, AXES, trade_map(axis, d)) for d in (1, 2, 3)]


def body(
    pair_rep,
    labels,
    residue_mask,
    dist_weight,
    dist_bias,
    bias_weight,
    query_scalar,
    query_points,
    key_scalar,
    key_points,
    value_scalar,
    value_points,
    point_weight,
    cot_scalar,
    cot_points,
    cot_pair,
):
    mask_rows = residue_mask.reshape(8, 128)
    weight_rows = jnp.transpose(dist_weight)
    bias_rows = jnp.transpose(bias_weight)

    own, same, other = own_logits(
        pair_rep, weight_rows, labels, (key_scalar, key_points, value_scalar, value_points)
    )
    same = lax.ppermute(same, AXES, FIRST_HOP)
    other = lax.ppermute(other, AXES, FIRST_HOP)
    pair_bias, pair_value, cot = pair_parts(pair_rep, cot_pair, bias_rows)
    same, pair_bias = lax.optimization_barrier((same, pair_bias))
    same = lax.ppermute(same, AXES, SECOND_HOP[0])
    other = lax.ppermute(other, AXES, SECOND_HOP[1])
    far_keys = lax.ppermute(same[SLABS:], AXES, CORE_SWAP)
    weights, value_grad, stats = attention_parts(
        (query_scalar, query_points, cot_scalar, cot_points),
        same,
        far_keys,
        pair_bias,
        pair_value,
        point_weight,
        mask_rows,
    )
    same, stats = lax.optimization_barrier((same, stats))
    bins, term = bin_gradient(
        pair_rep, own, same, other, labels, dist_bias.reshape(1, 64), mask_rows, residue_mask
    )
    message = packed(pack_kernel, BINS + STATS, "sum_cores", term, lax.ppermute(term, AXES, CORE_SWAP), stats)
    message = packed(pack_more_kernel, BINS + 2 * STATS, "sum_y", *trade(message, 1))
    arrived = trade(message, 0)
    own_sum, one, two, three = trade(packed(pack_more_kernel, BINS, "sum_x", *arrived), 2)
    pair_grad = pair_gradient(weights, value_grad, arrived, bins, cot, weight_rows, bias_rows)
    return (pair_grad, jnp.transpose((own_sum + two) + (one + three)))


def solution(mesh):
    placed = (
        P("row", "col", None),
        P("row", "col"),
        P(),
        P(),
        P(),
        P(),
        P("row", None),
        P("row", None),
        P("row", None),
        P("row", None),
        P("row", None),
        P("row", None),
        P(),
        P("row", None),
        P("row", None),
        P("row", None),
    )
    return jax.shard_map(
        body, mesh=mesh, in_specs=placed, out_specs=(P("row", "col", None), P()), check_vma=False
    )
```

```python
import functools
import math

import jax
import jax.numpy as jnp
import numpy as np
from jax import lax
from jax.experimental import pallas as pl
from jax.experimental.pallas import tpu as pltpu
from jax.sharding import PartitionSpec as P

AXES = ("row", "col")
LOGIT_WEIGHT = math.sqrt(1.0 / 3.0)
HEADS = 12
PAD_HEADS = 16
CHUNK = 8
QUANT = 32760.0
BINS = 64
STATS = 24

WIDTHS = (192, 144, 192, 288)
PER_HEAD = (16, 12, 16, 24)
CAT = 896
WINDOWS = ((0, 256), (128, 384), (256, 896))
WINDOW_PARTS = ((0,), (1,), (2, 3))

NT = (((1,), (1,)), ((), ()))
TN = (((0,), (0,)), ((), ()))

CHIPS = [(x, y, z) for x in range(4) for y in range(4) for z in range(4)]
Y_SWAP = (0, 2, 1, 3)


def device_index(chip, core):
    x, y, z = chip
    return ((y // 2) * 8 + z * 2 + core) * 8 + (y % 2) * 4 + x


def mirror_chip(chip):
    x, y, z = chip
    return (z, Y_SWAP[y], x)


def halfway_chip(chip, core):
    x, y, z = chip
    if core == 0:
        return (x, y, (x + z) % 4)
    return ((x + 3 * z + 2) % 4, Y_SWAP[y], x)


FIRST_HOP = [(device_index(n, h), device_index(halfway_chip(n, h), h)) for n in CHIPS for h in (0, 1)]
SECOND_HOP = [
    [
        (device_index(halfway_chip(n, h), h), device_index(mirror_chip(n), (h + s) % 2))
        for n in CHIPS
        for h in (0, 1)
    ]
    for s in (0, 1)
]
CORE_SWAP = [(device_index(n, h), device_index(n, 1 - h)) for n in CHIPS for h in (0, 1)]


def trade_map(axis, bits):
    pairs = []
    for n in CHIPS:
        m = list(n)
        m[axis] ^= bits
        pairs += [(device_index(n, h), device_index(tuple(m), 1 - h)) for h in (0, 1)]
    return pairs


def head_columns(lo, hi, parts):
    head = lax.broadcasted_iota(jnp.int32, (PAD_HEADS, hi - lo), 0)
    column = lax.broadcasted_iota(jnp.int32, (PAD_HEADS, hi - lo), 1) + lo
    held = jnp.zeros((PAD_HEADS, hi - lo), jnp.float32)
    for part in parts:
        size = PER_HEAD[part]
        first = sum(WIDTHS[:part]) + head * size
        inside = (column >= first) & (column < first + size) & (head < HEADS)
        held = jnp.where(inside, 1.0, held)
    return held


def dot(a, b, dims=(((1,), (0,)), ((), ()))):
    return lax.dot_general(a, b, dims, preferred_element_type=jnp.float32)


def eye(n, dtype):
    return (
        lax.broadcasted_iota(jnp.int32, (n, n), 0) == lax.broadcasted_iota(jnp.int32, (n, n), 1)
    ).astype(dtype)


def padded_heads(bias_ref):
    heads = bias_ref.shape[0]
    pick = (
        lax.broadcasted_iota(jnp.int32, (PAD_HEADS, heads), 0)
        == lax.broadcasted_iota(jnp.int32, (PAD_HEADS, heads), 1)
    ).astype(jnp.bfloat16)
    return dot(pick, bias_ref[...]).astype(jnp.bfloat16)


def own_core():
    return lax.rem(lax.axis_index("row"), 2)


def lay_out(cat_ref, parts):
    start = 0
    for part in parts:
        width = part.shape[1]
        cat_ref[:, start : start + width] = part[...]
        start += width
    cat_ref[:, start:] = jnp.zeros((cat_ref.shape[0], cat_ref.shape[1] - start), cat_ref.dtype)


def chunk_copies(source, target, arrived):
    count = arrived.shape[0]
    size = source.shape[0] // count
    return [
        pltpu.make_async_copy(
            source.at[pl.ds(k * size, size)], target.at[pl.ds(k * size, size)], arrived.at[k]
        )
        for k in range(count)
    ]


HBM = pl.BlockSpec(memory_space=pltpu.HBM)
VMEM = pl.BlockSpec(memory_space=pltpu.VMEM)
SMEM = pl.BlockSpec(memory_space=pltpu.SMEM)
PARAMS = pltpu.CompilerParams(vmem_limit_bytes=16 * 1024 * 1024)


SLABS = 33
KEY_SLABS = CAT // 128
SLAB_PARTS = ((0, 8), (8, 16), (16, 24), (24, 33))


def logits_kernel(pair_hbm, weight_hbm, labels_hbm, *refs):
    keys_hbm, (own_hbm, same_hbm, other_hbm) = refs[:4], refs[4:7]
    pair_ref, weight_ref, labels_ref, own_ref, same_ref, other_ref, cat_ref, slabs, top = refs[7:16]
    pair_sem, own_sem, slab_sem, small_sem = refs[16:20]
    keys_refs = refs[20:]
    copy = pltpu.make_async_copy
    weight_in = copy(weight_hbm, weight_ref, small_sem.at[0])
    small_in = [copy(labels_hbm, labels_ref, small_sem.at[1])]
    small_in += [copy(a, b, small_sem.at[3 + k]) for k, (a, b) in enumerate(zip(keys_hbm, keys_refs))]
    keys_out = copy(same_ref.at[pl.ds(SLABS, KEY_SLABS)], same_hbm.at[pl.ds(SLABS, KEY_SLABS)], small_sem.at[2])
    pair_in = chunk_copies(pair_hbm, pair_ref, pair_sem)
    own_out = chunk_copies(own_ref, own_hbm, own_sem)
    weight_in.start()
    for c in pair_in + small_in:
        c.start()
    weight_in.wait()
    weight_t = weight_ref[...]
    size = pair_ref.shape[0] // len(pair_in)
    for k in range(len(pair_in)):
        pair_in[k].wait()
        for first in range(k * size, (k + 1) * size, 4):
            flat = pair_ref[first : first + 4].reshape(4 * 128, 128)
            terms = dot(weight_t, flat, NT)
            for t in range(4):
                term = terms[:, t * 128 : (t + 1) * 128]
                row = first + t
                own_ref[row] = term
                slabs[pl.ds(row, 64, stride=64), :] = term
                top[pl.ds(row, 1), :] = jnp.max(jnp.abs(term), axis=0, keepdims=True)
        own_out[k].start()
    for c in small_in:
        c.wait()
    lay_out(cat_ref, keys_refs)

    def narrow(values):
        return jnp.clip(jnp.round(values), -32767.0, 32767.0).astype(jnp.int32).astype(jnp.int16)

    cat = cat_ref[...].astype(jnp.float32)
    column = lax.broadcasted_iota(jnp.int32, cat.shape, 1)
    coded = jnp.zeros_like(cat)
    for part, width in enumerate(WIDTHS):
        start = sum(WIDTHS[:part])
        held = (column >= start) & (column < start + width)
        largest = jnp.max(jnp.where(held, jnp.abs(cat), 0.0), axis=1, keepdims=True)
        part_level = jnp.ceil(16.0 * jnp.log2(jnp.maximum(largest, 1e-30)))
        coded = jnp.where(held, cat * (jnp.exp2(part_level * (-1.0 / 16.0)) * QUANT), coded)
        coded = jnp.where(column == sum(WIDTHS) + part, part_level, coded)
    coded = narrow(coded)
    for k in range(KEY_SLABS):
        same_ref[SLABS + k] = coded[:, k * 128 : (k + 1) * 128]
    keys_out.start()

    core = own_core()
    level = jnp.ceil(16.0 * jnp.log2(jnp.maximum(top[...], 1e-30)))
    scale = jnp.exp2(level * (-1.0 / 16.0)) * QUANT

    def put(slab, upper, lower):
        turned = jnp.transpose(jnp.concatenate([upper, lower], axis=0))
        first, second = turned[:64], turned[64:]
        same_ref[slab] = narrow(jnp.where(core == 0, first, second))
        other_ref[slab] = narrow(jnp.where(core == 0, second, first))

    slab_out = []
    for part, (lo, hi) in enumerate(SLAB_PARTS):
        for b in range(lo, min(hi, 32)):
            put(b, slabs[b * 64 : (b + 1) * 64, :] * scale, slabs[(b + 32) * 64 : (b + 33) * 64, :] * scale)
        if hi == SLABS:
            put(32, level, labels_ref[...].astype(jnp.float32))
        for k, (ref, hbm) in enumerate(((same_ref, same_hbm), (other_ref, other_hbm))):
            slab_out.append(copy(ref.at[pl.ds(lo, hi - lo)], hbm.at[pl.ds(lo, hi - lo)], slab_sem.at[part, k]))
            slab_out[-1].start()
    for c in own_out + slab_out + [keys_out]:
        c.wait()


def own_logits(pair_tile, weight_rows, labels, keys):
    rows = pair_tile.shape[0]
    same = jax.ShapeDtypeStruct((SLABS + KEY_SLABS, 64, 128), jnp.int16)
    other = jax.ShapeDtypeStruct((SLABS, 64, 128), jnp.int16)
    cat = jax.ShapeDtypeStruct((rows, CAT), jnp.bfloat16)
    own = jax.ShapeDtypeStruct((rows, 64, 128), jnp.float32)
    arrays = [pair_tile, weight_rows, labels, own, same, other, cat]
    return pl.pallas_call(
        logits_kernel,
        in_specs=[HBM] * (3 + len(keys)),
        out_specs=[HBM] * 3,
        out_shape=[own, same, other],
        scratch_shapes=[pltpu.VMEM(a.shape, a.dtype) for a in arrays]
        + [
            pltpu.VMEM((64 * 64, 128), jnp.float32),
            pltpu.VMEM((64, 128), jnp.float32),
            pltpu.SemaphoreType.DMA((4,)),
            pltpu.SemaphoreType.DMA((4,)),
            pltpu.SemaphoreType.DMA((len(SLAB_PARTS), 2)),
            pltpu.SemaphoreType.DMA((3 + len(keys),)),
        ]
        + [pltpu.VMEM(k.shape, k.dtype) for k in keys],
        compiler_params=pltpu.CompilerParams(vmem_limit_bytes=60 * 1024 * 1024),
        cost_estimate=pl.CostEstimate(flops=200_000_000, bytes_accessed=6_000_000, transcendentals=8192),
        name="own_logits",
    )(pair_tile, weight_rows, labels, *keys)


def pair_parts_kernel(pair_ref, cot_ref, bias_ref, bias_out_ref, value_out_ref, cot_out_ref, cot_rows):
    length = CHUNK * PAD_HEADS
    for h in range(HEADS):
        cot_rows[h * 64 : (h + 1) * 64] = cot_ref[:, h * 128 : (h + 1) * 128]
    bias_t = padded_heads(bias_ref)
    row_of = lax.broadcasted_iota(jnp.int32, (length, 768), 0)
    column_of = lax.broadcasted_iota(jnp.int32, (length, 768), 1)
    same_head = row_of % PAD_HEADS == column_of // 64
    place = column_of % 64 - row_of // PAD_HEADS
    for step in range(pair_ref.shape[0] // CHUNK):
        pick = (same_head & (place == step * CHUNK)).astype(jnp.bfloat16)
        cot = dot(pick, cot_rows[...]).astype(jnp.bfloat16)
        cot_out_ref[step * CHUNK : (step + 1) * CHUNK] = cot.reshape(CHUNK, PAD_HEADS, 128)
        for t in range(CHUNK):
            row = step * CHUNK + t
            both = jnp.concatenate([bias_t, cot[t * PAD_HEADS : (t + 1) * PAD_HEADS]], axis=0)
            result = dot(both, pair_ref[row], NT)
            bias_out_ref[row] = result[:PAD_HEADS]
            value_out_ref[row] = result[PAD_HEADS:]


def pair_parts(pair_tile, cot_pair, bias_rows):
    rows = pair_tile.shape[0]
    part = jax.ShapeDtypeStruct((rows, PAD_HEADS, 128), jnp.float32)
    return pl.pallas_call(
        pair_parts_kernel,
        in_specs=[VMEM] * 3,
        out_specs=[VMEM] * 3,
        out_shape=[part, part, jax.ShapeDtypeStruct((rows, PAD_HEADS, 128), jnp.bfloat16)],
        scratch_shapes=[pltpu.VMEM((768, 128), jnp.bfloat16)],
        compiler_params=PARAMS,
        cost_estimate=pl.CostEstimate(flops=300_000_000, bytes_accessed=4_000_000, transcendentals=0),
        name="pair_parts",
    )(pair_tile, cot_pair, bias_rows)


def attention_kernel(point_smem, near_ref, far_ref, pair_bias_ref, pair_value_ref, mask_ref, *refs):
    query_refs = refs[:4]
    exp_ref, grad_ref, stats_ref, keys, cat_ref = refs[4:]
    length = CHUNK * PAD_HEADS

    def iota(shape, dim):
        return lax.broadcasted_iota(jnp.int32, shape, dim)

    core = own_core()

    def decoded(ref, first):
        coded = jnp.concatenate(
            [ref[first + k].astype(jnp.int32).astype(jnp.float32) for k in range(KEY_SLABS)], axis=1
        )
        column = iota(coded.shape, 1)
        scale = jnp.zeros_like(coded)
        for part, width in enumerate(WIDTHS):
            start = sum(WIDTHS[:part])
            at = sum(WIDTHS) + part
            part_scale = jnp.exp2(coded[:, at : at + 1] * (1.0 / 16.0)) * (1.0 / QUANT)
            scale = jnp.where((column >= start) & (column < start + width), part_scale, scale)
        return coded * scale

    near, far = decoded(near_ref, SLABS), decoded(far_ref, 0)
    keys[:64] = jnp.where(core == 0, near, far).astype(jnp.bfloat16)
    keys[64:] = jnp.where(core == 0, far, near).astype(jnp.bfloat16)
    lay_out(cat_ref, query_refs)

    masks = [head_columns(lo, hi, parts) for (lo, hi), parts in zip(WINDOWS, WINDOW_PARTS)]
    right = [keys[:, lo:hi] for lo, hi in WINDOWS]
    key_points = right[1].astype(jnp.float32)
    key_sq = lax.dot_general(
        masks[1],
        key_points * key_points,
        NT,
        precision=lax.Precision.HIGHEST,
        preferred_element_type=jnp.float32,
    )
    key_sq = jnp.concatenate([key_sq] * CHUNK, axis=0)
    masks = [jnp.concatenate([mask] * CHUNK, axis=0) for mask in masks]

    head_of = iota((length, 128), 0) % PAD_HEADS
    raw = jnp.zeros((length, 128), jnp.float32)
    for h in range(HEADS):
        raw = jnp.where(head_of == h, point_smem[h], raw)
    softplus = jnp.maximum(raw, 0.0) + jnp.log1p(jnp.exp(-jnp.abs(raw)))
    point_scale = softplus * (math.sqrt(2.0 / 36.0) / 2.0)
    column_mask = mask_ref[pl.ds(lax.axis_index("col"), 1), :]
    key_bias = jnp.where(column_mask > 0, 0.0, -1000000000.0)
    lane = iota((length, 128), 1)
    place = iota((length, 64), 1) - iota((length, 64), 0) // PAD_HEADS

    for step in range(exp_ref.shape[0] // CHUNK):
        pick = (place == step * CHUNK).astype(jnp.bfloat16)
        spread = dot(pick, cat_ref[...])
        left = [spread[:, lo:hi] * mask for (lo, hi), mask in zip(WINDOWS, masks)]
        scalar_term, cross_term, value_term = [dot(a.astype(jnp.bfloat16), b, NT) for a, b in zip(left, right)]
        query_sq = jnp.sum(left[1] * left[1], axis=1, keepdims=True)
        rows = slice(step * CHUNK, (step + 1) * CHUNK)
        pair_bias = pair_bias_ref[rows].reshape(length, 128)
        value_grad = value_term + pair_value_ref[rows].reshape(length, 128)
        logits = (
            LOGIT_WEIGHT
            * (scalar_term * 0.25 + pair_bias - point_scale * (query_sq + key_sq - 2.0 * cross_term))
            + key_bias
        )
        top = jnp.max(logits, axis=1, keepdims=True)
        weights = jnp.exp(logits - top)
        total = jnp.sum(weights, axis=1, keepdims=True)
        weighted = jnp.sum(weights * value_grad, axis=1, keepdims=True)
        exp_ref[rows] = weights.reshape(CHUNK, PAD_HEADS, 128)
        grad_ref[rows] = value_grad.reshape(CHUNK, PAD_HEADS, 128)
        packed = jnp.where(lane == 0, top, jnp.where(lane == 1, total, jnp.where(lane == 2, weighted, 0.0)))
        packed = jnp.transpose(packed)
        for q in range(3):
            stats_ref[q * 8 + step : q * 8 + step + 1, :] = packed[q : q + 1]


def attention_parts(queries, near, far, pair_bias, pair_value, point_weight, mask_rows):
    part = jax.ShapeDtypeStruct(pair_bias.shape, jnp.float32)
    return pl.pallas_call(
        attention_kernel,
        in_specs=[SMEM] + [VMEM] * (5 + len(queries)),
        out_specs=[VMEM] * 3,
        out_shape=[part, part, jax.ShapeDtypeStruct((STATS, 128), jnp.float32)],
        scratch_shapes=[pltpu.VMEM((128, CAT), jnp.bfloat16), pltpu.VMEM((64, CAT), jnp.bfloat16)],
        compiler_params=PARAMS,
        cost_estimate=pl.CostEstimate(flops=500_000_000, bytes_accessed=2_000_000, transcendentals=200_000),
        name="attention_parts",
    )(point_weight, near, far, pair_bias, pair_value, mask_rows, *queries)


def bins_kernel(
    mask_smem, pair_ref, own_ref, labels_ref, near_ref, far_ref, bias_ref, mask_ref, stats_ref, bins_ref, weight_ref,
    mirror, mirror_labels,
):
    core = own_core()
    low_lanes = lax.broadcasted_iota(jnp.int32, (64, 128), 1) < 64

    def halves(slab):
        near = near_ref[slab].astype(jnp.int32).astype(jnp.float32)
        far = far_ref[slab].astype(jnp.int32).astype(jnp.float32)
        first = jnp.where(core == 0, near, far)
        second = jnp.where(core == 0, far, near)
        upper = jnp.where(low_lanes, first, pltpu.roll(second, 64, 1))
        lower = jnp.where(low_lanes, pltpu.roll(first, 64, 1), second)
        return upper, lower

    level, other_labels = halves(32)
    mirror_labels[...] = other_labels
    scale = jnp.exp2(level * (1.0 / 16.0)) * (1.0 / QUANT)

    def pair_of_bins(b, carry):
        upper, lower = halves(b)
        mirror[pl.ds(pl.multiple_of(b * 64, 64), 64), :] = upper * scale
        mirror[pl.ds(pl.multiple_of((b + 32) * 64, 64), 64), :] = lower * scale
        return carry

    lax.fori_loop(0, 32, pair_of_bins, 0, unroll=32)
    bias = jnp.sum(eye(64, jnp.float32) * bias_ref[...], axis=1, keepdims=True)
    bias = jnp.broadcast_to(bias, (64, 128))
    column_mask = mask_ref[pl.ds(lax.axis_index("col"), 1), :].astype(jnp.float32)
    bin_of = lax.broadcasted_iota(jnp.int32, (64, 128), 0)
    first_row = lax.axis_index("row") * 64

    total = jnp.zeros((64, 128), jnp.float32)
    for step in range(pair_ref.shape[0] // CHUNK):
        grads = []
        for t in range(CHUNK):
            row = step * CHUNK + t
            logits = own_ref[row] + mirror[pl.ds(row, 64, stride=64), :] + bias
            weights = jnp.exp(logits - jnp.max(logits, axis=0, keepdims=True))
            valid = column_mask * mask_smem[first_row + row].astype(jnp.float32)
            share = 2.0 * valid / jnp.sum(weights, axis=0, keepdims=True)
            own_label = labels_ref[pl.ds(row, 1), :]
            other_label = mirror_labels[pl.ds(row, 1), :].astype(jnp.int32)
            hits = jnp.where(bin_of == own_label, valid, 0.0) + jnp.where(bin_of == other_label, valid, 0.0)
            grad = (weights * share - hits).astype(jnp.bfloat16)
            bins_ref[row] = grad
            grads.append(grad)
        flat = pair_ref[step * CHUNK : (step + 1) * CHUNK].reshape(CHUNK * 128, 128)
        total += dot(jnp.concatenate(grads, axis=1), flat)
    weight_ref[:BINS] = total
    weight_ref[BINS:] = stats_ref[...]


def bin_gradient(pair_tile, own, near, far, labels, dist_bias, mask_rows, residue_mask, stats):
    rows = pair_tile.shape[0]
    return pl.pallas_call(
        bins_kernel,
        in_specs=[SMEM] + [VMEM] * 8,
        out_specs=[VMEM, VMEM],
        out_shape=[
            jax.ShapeDtypeStruct((rows, 64, 128), jnp.bfloat16),
            jax.ShapeDtypeStruct((BINS + STATS, 128), jnp.float32),
        ],
        scratch_shapes=[
            pltpu.VMEM((64 * 64, 128), jnp.float32),
            pltpu.VMEM((64, 128), jnp.float32),
        ],
        compiler_params=PARAMS,
        cost_estimate=pl.CostEstimate(flops=200_000_000, bytes_accessed=6_000_000, transcendentals=600_000),
        name="bin_gradient",
    )(residue_mask, pair_tile, own, labels, near, far, dist_bias, mask_rows, stats)


def output_kernel(exp_ref, grad_ref, *refs):
    core_ref, y_ref = refs[:2]
    x_refs, (bins_ref, cot_ref, weight_ref, bias_ref, out_hbm, out_ref, sent) = refs[2:5], refs[5:]
    length = CHUNK * PAD_HEADS
    weight_t = weight_ref[...]
    bias_t = padded_heads(bias_ref)
    places = [(core_ref, FIRST.start), (y_ref, SECOND.start)]
    places += [(ref, at.start) for ref in x_refs for at in (FIRST, SECOND)]
    tops = [ref[at : at + 8, :] for ref, at in places]
    totals = [ref[at + 8 : at + 16, :] for ref, at in places]
    weighted = [ref[at + 16 : at + 24, :] for ref, at in places]
    top = functools.reduce(jnp.maximum, tops)
    factors = [jnp.exp(m - top) for m in tops]
    total = sum(f * s for f, s in zip(factors, totals))
    means = sum(f * s for f, s in zip(factors, weighted)) / total
    shares = factors[0] / total
    going = chunk_copies(out_ref, out_hbm, sent)
    for step in range(out_ref.shape[0] // CHUNK):
        share = jnp.transpose(jnp.broadcast_to(shares[step : step + 1], (length, 128)))
        mean = jnp.transpose(jnp.broadcast_to(means[step : step + 1], (length, 128)))
        rows = slice(step * CHUNK, (step + 1) * CHUNK)
        attention = exp_ref[rows].reshape(length, 128) * share
        logit_grad = attention * (grad_ref[rows].reshape(length, 128) - mean)
        attention = attention.astype(jnp.bfloat16)
        logit_grad = (logit_grad * LOGIT_WEIGHT).astype(jnp.bfloat16)
        for t in range(CHUNK):
            heads = slice(t * PAD_HEADS, (t + 1) * PAD_HEADS)
            row = step * CHUNK + t
            left = jnp.concatenate([bins_ref[row], attention[heads], logit_grad[heads]], axis=0)
            right = jnp.concatenate([weight_t, cot_ref[row], bias_t], axis=0)
            out_ref[row] = dot(left, right, TN).astype(jnp.bfloat16)
        going[step].start()
    for copy in going:
        copy.wait()


def pair_gradient(weights, value_grad, stats, bins, cot, weight_rows, bias_rows):
    rows = bins.shape[0]
    return pl.pallas_call(
        output_kernel,
        in_specs=[VMEM] * 11,
        out_specs=HBM,
        out_shape=jax.ShapeDtypeStruct((rows, 128, 128), jnp.bfloat16),
        scratch_shapes=[
            pltpu.VMEM((rows, 128, 128), jnp.bfloat16),
            pltpu.SemaphoreType.DMA((rows // CHUNK,)),
        ],
        compiler_params=PARAMS,
        cost_estimate=pl.CostEstimate(flops=300_000_000, bytes_accessed=5_000_000, transcendentals=10_000),
        name="pair_gradient",
    )(weights, value_grad, *stats, bins, cot, weight_rows, bias_rows)


FIRST = slice(BINS, BINS + STATS)
SECOND = slice(BINS + STATS, BINS + 2 * STATS)


def pack_kernel(own_ref, swapped_ref, out_ref):
    out_ref[:BINS] = own_ref[:BINS] + swapped_ref[:BINS]
    out_ref[FIRST] = own_ref[FIRST]
    out_ref[SECOND] = swapped_ref[FIRST]


def pack_more_kernel(own_ref, one_ref, two_ref, three_ref, out_ref):
    out_ref[:BINS] = (own_ref[:BINS] + two_ref[:BINS]) + (one_ref[:BINS] + three_ref[:BINS])
    if out_ref.shape[0] > BINS:
        out_ref[FIRST] = own_ref[SECOND]
        out_ref[SECOND] = one_ref[FIRST]


def packed(kernel, rows, name, *arrays):
    return pl.pallas_call(
        kernel,
        in_specs=[VMEM] * len(arrays),
        out_specs=VMEM,
        out_shape=jax.ShapeDtypeStruct((rows, 128), jnp.float32),
        compiler_params=PARAMS,
        cost_estimate=pl.CostEstimate(flops=30_000, bytes_accessed=200_000, transcendentals=0),
        name=name,
    )(*arrays)


def trade(array, axis):
    return [array] + [lax.ppermute(array, AXES, trade_map(axis, d)) for d in (1, 2, 3)]


def body(
    pair_rep,
    labels,
    residue_mask,
    dist_weight,
    dist_bias,
    bias_weight,
    query_scalar,
    query_points,
    key_scalar,
    key_points,
    value_scalar,
    value_points,
    point_weight,
    cot_scalar,
    cot_points,
    cot_pair,
):
    mask_rows = residue_mask.reshape(8, 128)
    weight_rows = jnp.transpose(dist_weight)
    bias_rows = jnp.transpose(bias_weight)

    own, same, other = own_logits(
        pair_rep, weight_rows, labels, (key_scalar, key_points, value_scalar, value_points)
    )
    same = lax.ppermute(same, AXES, FIRST_HOP)
    other = lax.ppermute(other, AXES, FIRST_HOP)
    pair_bias, pair_value, cot = pair_parts(pair_rep, cot_pair, bias_rows)
    same, pair_bias = lax.optimization_barrier((same, pair_bias))
    same = lax.ppermute(same, AXES, SECOND_HOP[0])
    other = lax.ppermute(other, AXES, SECOND_HOP[1])
    far_keys = lax.ppermute(same[SLABS:], AXES, CORE_SWAP)
    weights, value_grad, stats = attention_parts(
        (query_scalar, query_points, cot_scalar, cot_points),
        same,
        far_keys,
        pair_bias,
        pair_value,
        point_weight,
        mask_rows,
    )
    bins, message = bin_gradient(
        pair_rep, own, same, other, labels, dist_bias.reshape(1, 64), mask_rows, residue_mask, stats
    )
    by_core = packed(pack_kernel, BINS + 2 * STATS, "sum_cores", message, lax.ppermute(message, AXES, CORE_SWAP))
    by_y = trade(by_core, 1)
    by_x = trade(packed(pack_more_kernel, BINS + 2 * STATS, "sum_y", *by_y), 0)
    own_sum, one, two, three = trade(packed(pack_more_kernel, BINS, "sum_x", *by_x), 2)
    stats = (by_core, by_y[1], *by_x[1:])
    pair_grad = pair_gradient(weights, value_grad, stats, bins, cot, weight_rows, bias_rows)
    return (pair_grad, jnp.transpose((own_sum + two) + (one + three)))


def solution(mesh):
    placed = (
        P("row", "col", None),
        P("row", "col"),
        P(),
        P(),
        P(),
        P(),
        P("row", None),
        P("row", None),
        P("row", None),
        P("row", None),
        P("row", None),
        P("row", None),
        P(),
        P("row", None),
        P("row", None),
        P("row", None),
    )
    return jax.shard_map(
        body, mesh=mesh, in_specs=placed, out_specs=(P("row", "col", None), P()), check_vma=False
    )
```

```python
import functools
import math

import jax
import jax.numpy as jnp
import numpy as np
from jax import lax
from jax.experimental import pallas as pl
from jax.experimental.pallas import tpu as pltpu
from jax.sharding import PartitionSpec as P

AXES = ("row", "col")
LOGIT_WEIGHT = math.sqrt(1.0 / 3.0)
HEADS = 12
PAD_HEADS = 16
CHUNK = 8
BIN_CHUNK = 16
QUANT = 32760.0
BINS = 64
STATS = 24

WIDTHS = (192, 144, 192, 288)
PER_HEAD = (16, 12, 16, 24)
CAT = 896
WINDOWS = ((0, 256), (128, 384), (256, 896))
WINDOW_PARTS = ((0,), (1,), (2, 3))

NT = (((1,), (1,)), ((), ()))
TN = (((0,), (0,)), ((), ()))

CHIPS = [(x, y, z) for x in range(4) for y in range(4) for z in range(4)]
Y_SWAP = (0, 2, 1, 3)


def device_index(chip, core):
    x, y, z = chip
    return ((y // 2) * 8 + z * 2 + core) * 8 + (y % 2) * 4 + x


def mirror_chip(chip):
    x, y, z = chip
    return (z, Y_SWAP[y], x)


def halfway_chip(chip, core):
    x, y, z = chip
    if core == 0:
        return (x, y, (x + z) % 4)
    return ((x + 3 * z + 2) % 4, Y_SWAP[y], x)


FIRST_HOP = [(device_index(n, h), device_index(halfway_chip(n, h), h)) for n in CHIPS for h in (0, 1)]
SECOND_HOP = [
    [
        (device_index(halfway_chip(n, h), h), device_index(mirror_chip(n), (h + s) % 2))
        for n in CHIPS
        for h in (0, 1)
    ]
    for s in (0, 1)
]
CORE_SWAP = [(device_index(n, h), device_index(n, 1 - h)) for n in CHIPS for h in (0, 1)]


def trade_map(axis, bits):
    pairs = []
    for n in CHIPS:
        m = list(n)
        m[axis] ^= bits
        pairs += [(device_index(n, h), device_index(tuple(m), 1 - h)) for h in (0, 1)]
    return pairs


def head_columns(lo, hi, parts):
    head = lax.broadcasted_iota(jnp.int32, (PAD_HEADS, hi - lo), 0)
    column = lax.broadcasted_iota(jnp.int32, (PAD_HEADS, hi - lo), 1) + lo
    held = jnp.zeros((PAD_HEADS, hi - lo), jnp.float32)
    for part in parts:
        size = PER_HEAD[part]
        first = sum(WIDTHS[:part]) + head * size
        inside = (column >= first) & (column < first + size) & (head < HEADS)
        held = jnp.where(inside, 1.0, held)
    return held


def dot(a, b, dims=(((1,), (0,)), ((), ()))):
    return lax.dot_general(a, b, dims, preferred_element_type=jnp.float32)


def eye(n, dtype):
    return (
        lax.broadcasted_iota(jnp.int32, (n, n), 0) == lax.broadcasted_iota(jnp.int32, (n, n), 1)
    ).astype(dtype)


def padded_heads(bias_ref):
    heads = bias_ref.shape[0]
    pick = (
        lax.broadcasted_iota(jnp.int32, (PAD_HEADS, heads), 0)
        == lax.broadcasted_iota(jnp.int32, (PAD_HEADS, heads), 1)
    ).astype(jnp.bfloat16)
    return dot(pick, bias_ref[...]).astype(jnp.bfloat16)


def own_core():
    return lax.rem(lax.axis_index("row"), 2)


def lay_out(cat_ref, parts):
    start = 0
    for part in parts:
        width = part.shape[1]
        cat_ref[:, start : start + width] = part[...]
        start += width
    cat_ref[:, start:] = jnp.zeros((cat_ref.shape[0], cat_ref.shape[1] - start), cat_ref.dtype)


def chunk_copies(source, target, arrived):
    count = arrived.shape[0]
    size = source.shape[0] // count
    return [
        pltpu.make_async_copy(
            source.at[pl.ds(k * size, size)], target.at[pl.ds(k * size, size)], arrived.at[k]
        )
        for k in range(count)
    ]


HBM = pl.BlockSpec(memory_space=pltpu.HBM)
VMEM = pl.BlockSpec(memory_space=pltpu.VMEM)
SMEM = pl.BlockSpec(memory_space=pltpu.SMEM)
PARAMS = pltpu.CompilerParams(vmem_limit_bytes=16 * 1024 * 1024)


SLABS = 33
KEY_SLABS = CAT // 128
SLAB_PARTS = ((0, 8), (8, 16), (16, 24), (24, 33))


def logits_kernel(pair_hbm, weight_hbm, labels_hbm, *refs):
    keys_hbm, (own_hbm, same_hbm, other_hbm) = refs[:4], refs[4:7]
    pair_ref, weight_ref, labels_ref, own_ref, same_ref, other_ref, cat_ref, slabs, top = refs[7:16]
    pair_sem, own_sem, slab_sem, small_sem = refs[16:20]
    keys_refs = refs[20:]
    copy = pltpu.make_async_copy
    weight_in = copy(weight_hbm, weight_ref, small_sem.at[0])
    small_in = [copy(labels_hbm, labels_ref, small_sem.at[1])]
    small_in += [copy(a, b, small_sem.at[3 + k]) for k, (a, b) in enumerate(zip(keys_hbm, keys_refs))]
    keys_out = copy(same_ref.at[pl.ds(SLABS, KEY_SLABS)], same_hbm.at[pl.ds(SLABS, KEY_SLABS)], small_sem.at[2])
    pair_in = chunk_copies(pair_hbm, pair_ref, pair_sem)
    own_out = chunk_copies(own_ref, own_hbm, own_sem)
    weight_in.start()
    for c in pair_in + small_in:
        c.start()
    weight_in.wait()
    weight_t = weight_ref[...]
    size = pair_ref.shape[0] // len(pair_in)
    for k in range(len(pair_in)):
        pair_in[k].wait()
        for first in range(k * size, (k + 1) * size, 4):
            flat = pair_ref[first : first + 4].reshape(4 * 128, 128)
            terms = dot(weight_t, flat, NT)
            for t in range(4):
                term = terms[:, t * 128 : (t + 1) * 128]
                row = first + t
                own_ref[row] = term
                slabs[pl.ds(row, 64, stride=64), :] = term
                top[pl.ds(row, 1), :] = jnp.max(jnp.abs(term), axis=0, keepdims=True)
        own_out[k].start()
    for c in small_in:
        c.wait()
    lay_out(cat_ref, keys_refs)

    def narrow(values):
        return jnp.clip(jnp.round(values), -32767.0, 32767.0).astype(jnp.int32).astype(jnp.int16)

    cat = cat_ref[...].astype(jnp.float32)
    column = lax.broadcasted_iota(jnp.int32, cat.shape, 1)
    coded = jnp.zeros_like(cat)
    for part, width in enumerate(WIDTHS):
        start = sum(WIDTHS[:part])
        held = (column >= start) & (column < start + width)
        largest = jnp.max(jnp.where(held, jnp.abs(cat), 0.0), axis=1, keepdims=True)
        part_level = jnp.ceil(16.0 * jnp.log2(jnp.maximum(largest, 1e-30)))
        coded = jnp.where(held, cat * (jnp.exp2(part_level * (-1.0 / 16.0)) * QUANT), coded)
        coded = jnp.where(column == sum(WIDTHS) + part, part_level, coded)
    coded = narrow(coded)
    for k in range(KEY_SLABS):
        same_ref[SLABS + k] = coded[:, k * 128 : (k + 1) * 128]
    keys_out.start()

    core = own_core()
    level = jnp.ceil(16.0 * jnp.log2(jnp.maximum(top[...], 1e-30)))
    scale = jnp.exp2(level * (-1.0 / 16.0)) * QUANT

    def put(slab, upper, lower):
        turned = jnp.transpose(jnp.concatenate([upper, lower], axis=0))
        first, second = turned[:64], turned[64:]
        same_ref[slab] = narrow(jnp.where(core == 0, first, second))
        other_ref[slab] = narrow(jnp.where(core == 0, second, first))

    slab_out = []
    for part, (lo, hi) in enumerate(SLAB_PARTS):
        for b in range(lo, min(hi, 32)):
            put(b, slabs[b * 64 : (b + 1) * 64, :] * scale, slabs[(b + 32) * 64 : (b + 33) * 64, :] * scale)
        if hi == SLABS:
            put(32, level, labels_ref[...].astype(jnp.float32))
        for k, (ref, hbm) in enumerate(((same_ref, same_hbm), (other_ref, other_hbm))):
            slab_out.append(copy(ref.at[pl.ds(lo, hi - lo)], hbm.at[pl.ds(lo, hi - lo)], slab_sem.at[part, k]))
            slab_out[-1].start()
    for c in own_out + slab_out + [keys_out]:
        c.wait()


def own_logits(pair_tile, weight_rows, labels, keys):
    rows = pair_tile.shape[0]
    same = jax.ShapeDtypeStruct((SLABS + KEY_SLABS, 64, 128), jnp.int16)
    other = jax.ShapeDtypeStruct((SLABS, 64, 128), jnp.int16)
    cat = jax.ShapeDtypeStruct((rows, CAT), jnp.bfloat16)
    own = jax.ShapeDtypeStruct((rows, 64, 128), jnp.float32)
    arrays = [pair_tile, weight_rows, labels, own, same, other, cat]
    return pl.pallas_call(
        logits_kernel,
        in_specs=[HBM] * (3 + len(keys)),
        out_specs=[HBM] * 3,
        out_shape=[own, same, other],
        scratch_shapes=[pltpu.VMEM(a.shape, a.dtype) for a in arrays]
        + [
            pltpu.VMEM((64 * 64, 128), jnp.float32),
            pltpu.VMEM((64, 128), jnp.float32),
            pltpu.SemaphoreType.DMA((4,)),
            pltpu.SemaphoreType.DMA((4,)),
            pltpu.SemaphoreType.DMA((len(SLAB_PARTS), 2)),
            pltpu.SemaphoreType.DMA((3 + len(keys),)),
        ]
        + [pltpu.VMEM(k.shape, k.dtype) for k in keys],
        compiler_params=pltpu.CompilerParams(vmem_limit_bytes=60 * 1024 * 1024),
        cost_estimate=pl.CostEstimate(flops=200_000_000, bytes_accessed=6_000_000, transcendentals=8192),
        name="own_logits",
    )(pair_tile, weight_rows, labels, *keys)


def pair_parts_kernel(pair_ref, cot_ref, bias_ref, bias_out_ref, value_out_ref, cot_out_ref, cot_rows):
    length = CHUNK * PAD_HEADS
    for h in range(HEADS):
        cot_rows[h * 64 : (h + 1) * 64] = cot_ref[:, h * 128 : (h + 1) * 128]
    bias_t = padded_heads(bias_ref)
    row_of = lax.broadcasted_iota(jnp.int32, (length, 768), 0)
    column_of = lax.broadcasted_iota(jnp.int32, (length, 768), 1)
    same_head = row_of % PAD_HEADS == column_of // 64
    place = column_of % 64 - row_of // PAD_HEADS
    for step in range(pair_ref.shape[0] // CHUNK):
        pick = (same_head & (place == step * CHUNK)).astype(jnp.bfloat16)
        cot = dot(pick, cot_rows[...]).astype(jnp.bfloat16)
        cot_out_ref[step * CHUNK : (step + 1) * CHUNK] = cot.reshape(CHUNK, PAD_HEADS, 128)
        for t in range(CHUNK):
            row = step * CHUNK + t
            both = jnp.concatenate([bias_t, cot[t * PAD_HEADS : (t + 1) * PAD_HEADS]], axis=0)
            result = dot(both, pair_ref[row], NT)
            bias_out_ref[row] = result[:PAD_HEADS]
            value_out_ref[row] = result[PAD_HEADS:]


def pair_parts(pair_tile, cot_pair, bias_rows):
    rows = pair_tile.shape[0]
    part = jax.ShapeDtypeStruct((rows, PAD_HEADS, 128), jnp.float32)
    return pl.pallas_call(
        pair_parts_kernel,
        in_specs=[VMEM] * 3,
        out_specs=[VMEM] * 3,
        out_shape=[part, part, jax.ShapeDtypeStruct((rows, PAD_HEADS, 128), jnp.bfloat16)],
        scratch_shapes=[pltpu.VMEM((768, 128), jnp.bfloat16)],
        compiler_params=PARAMS,
        cost_estimate=pl.CostEstimate(flops=300_000_000, bytes_accessed=4_000_000, transcendentals=0),
        name="pair_parts",
    )(pair_tile, cot_pair, bias_rows)


def attention_kernel(point_smem, near_ref, far_ref, pair_bias_ref, pair_value_ref, mask_ref, *refs):
    query_refs = refs[:4]
    exp_ref, grad_ref, stats_ref, keys, cat_ref = refs[4:]
    length = CHUNK * PAD_HEADS

    def iota(shape, dim):
        return lax.broadcasted_iota(jnp.int32, shape, dim)

    core = own_core()

    def decoded(ref, first):
        coded = jnp.concatenate(
            [ref[first + k].astype(jnp.int32).astype(jnp.float32) for k in range(KEY_SLABS)], axis=1
        )
        column = iota(coded.shape, 1)
        scale = jnp.zeros_like(coded)
        for part, width in enumerate(WIDTHS):
            start = sum(WIDTHS[:part])
            at = sum(WIDTHS) + part
            part_scale = jnp.exp2(coded[:, at : at + 1] * (1.0 / 16.0)) * (1.0 / QUANT)
            scale = jnp.where((column >= start) & (column < start + width), part_scale, scale)
        return coded * scale

    near, far = decoded(near_ref, SLABS), decoded(far_ref, 0)
    keys[:64] = jnp.where(core == 0, near, far).astype(jnp.bfloat16)
    keys[64:] = jnp.where(core == 0, far, near).astype(jnp.bfloat16)
    lay_out(cat_ref, query_refs)

    masks = [head_columns(lo, hi, parts) for (lo, hi), parts in zip(WINDOWS, WINDOW_PARTS)]
    right = [keys[:, lo:hi] for lo, hi in WINDOWS]
    key_points = right[1].astype(jnp.float32)
    key_sq = lax.dot_general(
        masks[1],
        key_points * key_points,
        NT,
        precision=lax.Precision.HIGHEST,
        preferred_element_type=jnp.float32,
    )
    key_sq = jnp.concatenate([key_sq] * CHUNK, axis=0)
    masks = [jnp.concatenate([mask] * CHUNK, axis=0) for mask in masks]

    head_of = iota((length, 128), 0) % PAD_HEADS
    raw = jnp.zeros((length, 128), jnp.float32)
    for h in range(HEADS):
        raw = jnp.where(head_of == h, point_smem[h], raw)
    softplus = jnp.maximum(raw, 0.0) + jnp.log1p(jnp.exp(-jnp.abs(raw)))
    point_scale = softplus * (math.sqrt(2.0 / 36.0) / 2.0)
    column_mask = mask_ref[pl.ds(lax.axis_index("col"), 1), :]
    key_bias = jnp.where(column_mask > 0, 0.0, -1000000000.0)
    lane = iota((length, 128), 1)
    place = iota((length, 64), 1) - iota((length, 64), 0) // PAD_HEADS

    for step in range(exp_ref.shape[0] // CHUNK):
        pick = (place == step * CHUNK).astype(jnp.bfloat16)
        spread = dot(pick, cat_ref[...])
        left = [spread[:, lo:hi] * mask for (lo, hi), mask in zip(WINDOWS, masks)]
        scalar_term, cross_term, value_term = [dot(a.astype(jnp.bfloat16), b, NT) for a, b in zip(left, right)]
        query_sq = jnp.sum(left[1] * left[1], axis=1, keepdims=True)
        rows = slice(step * CHUNK, (step + 1) * CHUNK)
        pair_bias = pair_bias_ref[rows].reshape(length, 128)
        value_grad = value_term + pair_value_ref[rows].reshape(length, 128)
        logits = (
            LOGIT_WEIGHT
            * (scalar_term * 0.25 + pair_bias - point_scale * (query_sq + key_sq - 2.0 * cross_term))
            + key_bias
        )
        top = jnp.max(logits, axis=1, keepdims=True)
        weights = jnp.exp(logits - top)
        total = jnp.sum(weights, axis=1, keepdims=True)
        weighted = jnp.sum(weights * value_grad, axis=1, keepdims=True)
        exp_ref[rows] = weights.reshape(CHUNK, PAD_HEADS, 128)
        grad_ref[rows] = value_grad.reshape(CHUNK, PAD_HEADS, 128)
        packed = jnp.where(lane == 0, top, jnp.where(lane == 1, total, jnp.where(lane == 2, weighted, 0.0)))
        packed = jnp.transpose(packed)
        for q in range(3):
            stats_ref[q * 8 + step : q * 8 + step + 1, :] = packed[q : q + 1]


def attention_parts(queries, near, far, pair_bias, pair_value, point_weight, mask_rows):
    part = jax.ShapeDtypeStruct(pair_bias.shape, jnp.float32)
    return pl.pallas_call(
        attention_kernel,
        in_specs=[SMEM] + [VMEM] * (5 + len(queries)),
        out_specs=[VMEM] * 3,
        out_shape=[part, part, jax.ShapeDtypeStruct((STATS, 128), jnp.float32)],
        scratch_shapes=[pltpu.VMEM((128, CAT), jnp.bfloat16), pltpu.VMEM((64, CAT), jnp.bfloat16)],
        compiler_params=PARAMS,
        cost_estimate=pl.CostEstimate(flops=500_000_000, bytes_accessed=2_000_000, transcendentals=200_000),
        name="attention_parts",
    )(point_weight, near, far, pair_bias, pair_value, mask_rows, *queries)


def bins_kernel(
    mask_smem, pair_ref, own_ref, labels_ref, near_ref, far_ref, bias_ref, mask_ref, stats_ref, bins_ref, weight_ref,
    mirror, mirror_labels,
):
    core = own_core()
    low_lanes = lax.broadcasted_iota(jnp.int32, (64, 128), 1) < 64

    def halves(slab):
        near, far = near_ref[slab], far_ref[slab]
        first = lax.select(core == 0, near, far).astype(jnp.int32).astype(jnp.float32)
        second = lax.select(core == 0, far, near).astype(jnp.int32).astype(jnp.float32)
        upper = jnp.where(low_lanes, first, pltpu.roll(second, 64, 1))
        lower = jnp.where(low_lanes, pltpu.roll(first, 64, 1), second)
        return upper, lower

    level, other_labels = halves(32)
    mirror_labels[...] = other_labels
    scale = jnp.exp2(level * (1.0 / 16.0)) * (1.0 / QUANT)

    def pair_of_bins(b, carry):
        upper, lower = halves(b)
        mirror[pl.ds(pl.multiple_of(b * 64, 64), 64), :] = upper * scale
        mirror[pl.ds(pl.multiple_of((b + 32) * 64, 64), 64), :] = lower * scale
        return carry

    lax.fori_loop(0, 32, pair_of_bins, 0, unroll=32)
    bias = jnp.sum(eye(64, jnp.float32) * bias_ref[...], axis=1, keepdims=True)
    bias = jnp.broadcast_to(bias, (64, 128))
    column_mask = mask_ref[pl.ds(lax.axis_index("col"), 1), :].astype(jnp.float32)
    bin_of = lax.broadcasted_iota(jnp.int32, (64, 128), 0)
    first_row = lax.axis_index("row") * 64

    total = jnp.zeros((64, 128), jnp.float32)
    for step in range(pair_ref.shape[0] // BIN_CHUNK):
        grads = []
        for t in range(BIN_CHUNK):
            row = step * BIN_CHUNK + t
            logits = own_ref[row] + mirror[pl.ds(row, 64, stride=64), :] + bias
            weights = jnp.exp(logits - jnp.max(logits, axis=0, keepdims=True))
            valid = column_mask * mask_smem[first_row + row].astype(jnp.float32)
            share = 2.0 * valid / jnp.sum(weights, axis=0, keepdims=True)
            own_label = labels_ref[pl.ds(row, 1), :]
            other_label = mirror_labels[pl.ds(row, 1), :].astype(jnp.int32)
            hits = jnp.where(bin_of == own_label, valid, 0.0) + jnp.where(bin_of == other_label, valid, 0.0)
            grad = (weights * share - hits).astype(jnp.bfloat16)
            bins_ref[row] = grad
            grads.append(grad)
        flat = pair_ref[step * BIN_CHUNK : (step + 1) * BIN_CHUNK].reshape(BIN_CHUNK * 128, 128)
        total += dot(jnp.concatenate(grads, axis=1), flat)
    weight_ref[:BINS] = total
    weight_ref[BINS:] = stats_ref[...]


def bin_gradient(pair_tile, own, near, far, labels, dist_bias, mask_rows, residue_mask, stats):
    rows = pair_tile.shape[0]
    return pl.pallas_call(
        bins_kernel,
        in_specs=[SMEM] + [VMEM] * 8,
        out_specs=[VMEM, VMEM],
        out_shape=[
            jax.ShapeDtypeStruct((rows, 64, 128), jnp.bfloat16),
            jax.ShapeDtypeStruct((BINS + STATS, 128), jnp.float32),
        ],
        scratch_shapes=[
            pltpu.VMEM((64 * 64, 128), jnp.float32),
            pltpu.VMEM((64, 128), jnp.float32),
        ],
        compiler_params=PARAMS,
        cost_estimate=pl.CostEstimate(flops=200_000_000, bytes_accessed=6_000_000, transcendentals=600_000),
        name="bin_gradient",
    )(residue_mask, pair_tile, own, labels, near, far, dist_bias, mask_rows, stats)


def output_kernel(exp_ref, grad_ref, *refs):
    core_ref, y_ref = refs[:2]
    x_refs, (bins_ref, cot_ref, weight_ref, bias_ref, out_hbm, out_ref, sent) = refs[2:5], refs[5:]
    length = CHUNK * PAD_HEADS
    weight_t = weight_ref[...]
    bias_t = padded_heads(bias_ref)
    places = [(core_ref, FIRST.start), (y_ref, SECOND.start)]
    places += [(ref, at.start) for ref in x_refs for at in (FIRST, SECOND)]
    tops = [ref[at : at + 8, :] for ref, at in places]
    totals = [ref[at + 8 : at + 16, :] for ref, at in places]
    weighted = [ref[at + 16 : at + 24, :] for ref, at in places]
    top = functools.reduce(jnp.maximum, tops)
    factors = [jnp.exp(m - top) for m in tops]
    total = sum(f * s for f, s in zip(factors, totals))
    means = sum(f * s for f, s in zip(factors, weighted)) / total
    shares = factors[0] / total
    going = chunk_copies(out_ref, out_hbm, sent)
    for step in range(out_ref.shape[0] // CHUNK):
        share = jnp.transpose(jnp.broadcast_to(shares[step : step + 1], (length, 128)))
        mean = jnp.transpose(jnp.broadcast_to(means[step : step + 1], (length, 128)))
        rows = slice(step * CHUNK, (step + 1) * CHUNK)
        attention = exp_ref[rows].reshape(length, 128) * share
        logit_grad = attention * (grad_ref[rows].reshape(length, 128) - mean)
        attention = attention.astype(jnp.bfloat16)
        logit_grad = (logit_grad * LOGIT_WEIGHT).astype(jnp.bfloat16)
        for t in range(CHUNK):
            heads = slice(t * PAD_HEADS, (t + 1) * PAD_HEADS)
            row = step * CHUNK + t
            left = jnp.concatenate([bins_ref[row], attention[heads], logit_grad[heads]], axis=0)
            right = jnp.concatenate([weight_t, cot_ref[row], bias_t], axis=0)
            out_ref[row] = dot(left, right, TN).astype(jnp.bfloat16)
        going[step].start()
    for copy in going:
        copy.wait()


def pair_gradient(weights, value_grad, stats, bins, cot, weight_rows, bias_rows):
    rows = bins.shape[0]
    return pl.pallas_call(
        output_kernel,
        in_specs=[VMEM] * 11,
        out_specs=HBM,
        out_shape=jax.ShapeDtypeStruct((rows, 128, 128), jnp.bfloat16),
        scratch_shapes=[
            pltpu.VMEM((rows, 128, 128), jnp.bfloat16),
            pltpu.SemaphoreType.DMA((rows // CHUNK,)),
        ],
        compiler_params=PARAMS,
        cost_estimate=pl.CostEstimate(flops=300_000_000, bytes_accessed=5_000_000, transcendentals=10_000),
        name="pair_gradient",
    )(weights, value_grad, *stats, bins, cot, weight_rows, bias_rows)


FIRST = slice(BINS, BINS + STATS)
SECOND = slice(BINS + STATS, BINS + 2 * STATS)


def pack_kernel(own_ref, swapped_ref, out_ref):
    out_ref[:BINS] = own_ref[:BINS] + swapped_ref[:BINS]
    out_ref[FIRST] = own_ref[FIRST]
    out_ref[SECOND] = swapped_ref[FIRST]


def pack_more_kernel(own_ref, one_ref, two_ref, three_ref, out_ref):
    out_ref[:BINS] = (own_ref[:BINS] + two_ref[:BINS]) + (one_ref[:BINS] + three_ref[:BINS])
    if out_ref.shape[0] > BINS:
        out_ref[FIRST] = own_ref[SECOND]
        out_ref[SECOND] = one_ref[FIRST]


def packed(kernel, rows, name, *arrays):
    return pl.pallas_call(
        kernel,
        in_specs=[VMEM] * len(arrays),
        out_specs=VMEM,
        out_shape=jax.ShapeDtypeStruct((rows, 128), jnp.float32),
        compiler_params=PARAMS,
        cost_estimate=pl.CostEstimate(flops=30_000, bytes_accessed=200_000, transcendentals=0),
        name=name,
    )(*arrays)


def trade(array, axis):
    return [array] + [lax.ppermute(array, AXES, trade_map(axis, d)) for d in (1, 2, 3)]


def body(
    pair_rep,
    labels,
    residue_mask,
    dist_weight,
    dist_bias,
    bias_weight,
    query_scalar,
    query_points,
    key_scalar,
    key_points,
    value_scalar,
    value_points,
    point_weight,
    cot_scalar,
    cot_points,
    cot_pair,
):
    mask_rows = residue_mask.reshape(8, 128)
    weight_rows = jnp.transpose(dist_weight)
    bias_rows = jnp.transpose(bias_weight)

    own, same, other = own_logits(
        pair_rep, weight_rows, labels, (key_scalar, key_points, value_scalar, value_points)
    )
    same = lax.ppermute(same, AXES, FIRST_HOP)
    other = lax.ppermute(other, AXES, FIRST_HOP)
    pair_bias, pair_value, cot = pair_parts(pair_rep, cot_pair, bias_rows)
    same, pair_bias = lax.optimization_barrier((same, pair_bias))
    same = lax.ppermute(same, AXES, SECOND_HOP[0])
    other = lax.ppermute(other, AXES, SECOND_HOP[1])
    far_keys = lax.ppermute(same[SLABS:], AXES, CORE_SWAP)
    weights, value_grad, stats = attention_parts(
        (query_scalar, query_points, cot_scalar, cot_points),
        same,
        far_keys,
        pair_bias,
        pair_value,
        point_weight,
        mask_rows,
    )
    bins, message = bin_gradient(
        pair_rep, own, same, other, labels, dist_bias.reshape(1, 64), mask_rows, residue_mask, stats
    )
    by_core = packed(pack_kernel, BINS + 2 * STATS, "sum_cores", message, lax.ppermute(message, AXES, CORE_SWAP))
    by_y = trade(by_core, 1)
    by_x = trade(packed(pack_more_kernel, BINS + 2 * STATS, "sum_y", *by_y), 0)
    own_sum, one, two, three = trade(packed(pack_more_kernel, BINS, "sum_x", *by_x), 2)
    stats = (by_core, by_y[1], *by_x[1:])
    pair_grad = pair_gradient(weights, value_grad, stats, bins, cot, weight_rows, bias_rows)
    return (pair_grad, jnp.transpose((own_sum + two) + (one + three)))


def solution(mesh):
    placed = (
        P("row", "col", None),
        P("row", "col"),
        P(),
        P(),
        P(),
        P(),
        P("row", None),
        P("row", None),
        P("row", None),
        P("row", None),
        P("row", None),
        P("row", None),
        P(),
        P("row", None),
        P("row", None),
        P("row", None),
    )
    return jax.shard_map(
        body, mesh=mesh, in_specs=placed, out_specs=(P("row", "col", None), P()), check_vma=False
    )
```
